32 devices in a mesh: bin: 8 (over y, x, core), shard: 4 (over z).
Axes of the slice: x: 2, y: 2, z: 4, core: 2. Of those that a mesh axis runs over, the one named last changes fastest.
Arguments:
- block_input: bfloat16 [16384, 1152], P(('bin', 'shard')), may hold values from -6 to 6
- label_embed: float32 [64, 1152], P('bin'), may hold values from -6 to 6
- time_index: int32 [64], P('bin'), may hold values from 0 to 999
- segment_ids: int32 [16384], P('bin'), may hold values from 0 to 7, as said below
- ada_weight: bfloat16 [1152, 6912], replicated, may hold values from -0.1875 to 0.1875
- ada_bias: float32 [6912], replicated, may hold values from -2 to 2
- qkv_weight: bfloat16 [1152, 3456], P('bin', 'shard'), may hold values from -0.1875 to 0.1875
- qv_bias: float32 [2304], replicated, may hold values from -2 to 2
- proj_weight: bfloat16 [1152, 1152], P('bin', 'shard'), may hold values from -0.75 to 0.75
- proj_bias: float32 [1152], replicated, may hold values from -2 to 2
- up_weight: bfloat16 [1152, 4608], P('bin', 'shard'), may hold values from -0.1875 to 0.1875
- up_bias: float32 [4608], replicated, may hold values from -2 to 2
- down_weight: bfloat16 [4608, 1152], P('bin', 'shard'), may hold values from -0.09375 to 0.09375
- down_bias: float32 [1152], replicated, may hold values from -2 to 2
- bin_weight: float32 [8], P('bin'), may hold values from 0.3 to 3
- out_cotangent: bfloat16 [16384, 1152], P(('bin', 'shard')), may hold values from -6 to 6
Outputs:
- block_output: float32 [16384, 1152], P(('bin', 'shard'))
- grad_input: float32 [16384, 1152], P(('bin', 'shard'))
- grad_label: float32 [64, 1152], P('bin')
- grad_ada_weight: float32 [1152, 6912], P(None, ('bin', 'shard'))
- grad_ada_bias: float32 [6912], P(('bin', 'shard'))
- grad_qkv_weight: float32 [1152, 3456], P('bin', 'shard')
- grad_qv_bias: float32 [2304], replicated
- grad_proj_weight: float32 [1152, 1152], P('bin', 'shard')
- grad_proj_bias: float32 [1152], replicated
- grad_up_weight: float32 [1152, 4608], P('bin', 'shard')
- grad_up_bias: float32 [4608], replicated
- grad_down_weight: float32 [4608, 1152], P('bin', 'shard')
- grad_down_bias: float32 [1152], replicated
The draws below stay inside these ranges and needn't reach their ends.
Inputs may be any that keep to these rules, and one draw needn't show every extreme that they name: `segment_ids`: within each bin's group of 2048 tokens the ids number its images from 0 in order of their tokens; every image is 256 or 1024 consecutive tokens, and both sizes occur in every draw. Slots at or above a group's image count are unused.
All inputs are finite; a program needn't handle non-finite values.
Results may differ from the reference program's by a relative error of at most 0.017.
Values may be sent and summed in bfloat16 or wider, within the bound.
No kernel may reach another device: no remote copies, remote signals or barrier semaphores. Data moves between devices by JAX's collectives and lax.ppermute only.
A program may use at most 384 MiB of HBM per device.

```python
import math
import jax
import jax.numpy as jnp
from jax import lax

D = 1152
HEADS = 16
HEAD_DIM = 72
FF = 4608
IMG_SHORT = 256
BINS = 8
GROUP_TOK = 2048
IMG_GRP = 8
TOKENS = 16384
IMAGES = 64


def draw_segment_ids(key, part):
    units = GROUP_TOK // IMG_SHORT
    quads = units // 4
    key_long, key_lead = jax.random.split(jax.random.fold_in(key, 7))
    long_flags = jax.random.randint(key_long, (BINS, quads), 0, 2)
    leading = jax.random.randint(key_lead, (BINS,), 0, 4)
    group_pos = jnp.arange(BINS)
    long_flags = jnp.where(group_pos[:, None] == 0, 0, long_flags)
    long_flags = jnp.where(group_pos[:, None] == 1, 1, long_flags)
    unit_pos = jnp.arange(units)
    inner = unit_pos[None, :] - leading[:, None]
    quad_index = jnp.clip(inner // 4, 0, quads - 1)
    in_middle = (inner >= 0) & (inner < 4 * (quads - 1))
    flagged = jnp.take_along_axis(long_flags, quad_index, axis=1)
    is_long = in_middle & (flagged == 1)
    starts = jnp.where(is_long & (inner % 4 != 0), 0, 1)
    unit_segments = jnp.cumsum(starts, axis=1) - 1
    return jnp.repeat(unit_segments, IMG_SHORT, axis=1).reshape(-1).astype(jnp.int32)


def with_ends(result, rng, least, high):
    spot = [jax.random.randint(jax.random.fold_in(rng, axis), (), 0, length) for axis, length in enumerate(result.shape)]
    main_axis = result.shape.index(max(result.shape))
    neighbour = spot[:main_axis] + [(spot[main_axis] + 1) % result.shape[main_axis]] + spot[main_axis + 1:]
    return result.at[tuple(spot)].set(least).at[tuple(neighbour)].set(high)


def shard_levels(stream_key, dims, cuts, low, largest):
    factor_of = 1.0
    for axis_at, parts in cuts:
        heights = jax.random.uniform(jax.random.fold_in(jax.random.fold_in(stream_key, 6), axis_at), (parts,), jnp.float32, low / len(cuts), largest / len(cuts))
        factor_of = factor_of * jnp.repeat(jnp.exp(heights), dims[axis_at] // parts).reshape((-1,) + (1,) * (len(dims) - 1 - axis_at))
    return factor_of


def normal_values(key, shape, scale, limit, pieces=(), kind=jnp.bfloat16):
    drawn = jax.random.normal(key, shape, jnp.float32) * scale
    if len(pieces) > 0:
        drawn = shard_levels(key, shape, pieces, -0.22, 0.18) * drawn
    return jnp.clip(drawn, min=-limit, max=limit).astype(kind)


def setup_inputs(seed: int = 0) -> dict:
    seeds = jax.random.split(jax.random.key(seed), 17)
    return {
        "block_input": normal_values(seeds[0], (TOKENS, D), 1.0, 6.0, ((0, 32),)),
        "label_embed": normal_values(seeds[1], (IMAGES, D), 1.0, 6.0, ((0, 8),), jnp.float32),
        "time_index": with_ends(jax.random.randint(seeds[2], (IMAGES,), 0, 1000), jax.random.fold_in(seeds[2], 1), 0, 999).astype(jnp.int32),
        "segment_ids": draw_segment_ids(jax.random.fold_in(seeds[16], 71), 0),
        "ada_weight": normal_values(seeds[4], (D, 6 * D), D ** -0.5, 0.1875),
        "ada_bias": normal_values(seeds[5], (6 * D,), 0.3, 2.0, (), jnp.float32),
        "qkv_weight": normal_values(seeds[6], (D, 3 * D), D ** -0.5, 0.1875, ((0, 8), (1, 4))),
        "qv_bias": normal_values(seeds[7], (2 * D,), 0.3, 2.0, (), jnp.float32),
        "proj_weight": normal_values(seeds[8], (D, D), (D // 16) ** -0.5, 0.75, ((0, 8), (1, 4))),
        "proj_bias": normal_values(seeds[9], (D,), 0.3, 2.0, (), jnp.float32),
        "up_weight": normal_values(seeds[10], (D, FF), D ** -0.5, 0.1875, ((0, 8), (1, 4))),
        "up_bias": normal_values(seeds[11], (FF,), 0.3, 2.0, (), jnp.float32),
        "down_weight": normal_values(seeds[12], (FF, D), FF ** -0.5, 0.09375, ((0, 8), (1, 4))),
        "down_bias": normal_values(seeds[13], (D,), 0.3, 2.0, (), jnp.float32),
        "bin_weight": jnp.clip(jnp.exp(math.log(3.0) - 2.3025851 * jax.random.uniform(seeds[14], (BINS,), jnp.float32) ** shard_levels(seeds[14], (BINS,), ((0, 8),), -0.2, 0.2)), 0.3, 3.0),
        "out_cotangent": normal_values(seeds[15], (TOKENS, D), 1.0, 6.0, ((0, 32),)),
    }


@jax.custom_vjp
def low(v):
    return lax.optimization_barrier(v.astype(jnp.bfloat16)).astype(jnp.float32)

@jax.custom_vjp
def low_back(v):
    return v

def low_keep(v):
    return (low(v), None)

def low_pass(kept, grad):
    return (grad,)

def back_keep(v):
    return (v, None)

def back_low(kept, grad):
    return (low(grad),)
low.defvjp(low_keep, low_pass)
low_back.defvjp(back_keep, back_low)

def product(left, right):
    return jnp.dot(left, right, precision=lax.Precision.HIGHEST, preferred_element_type=jnp.float32)

def time_embed(time_index, width):
    half_width = width // 2
    freqs = jnp.exp(-math.log(10000.0) * jnp.arange(half_width, dtype=jnp.float32) / half_width)
    angles = time_index.astype(jnp.float32)[:, None] * freqs[None, :]
    return jnp.concatenate([jnp.cos(angles), jnp.sin(angles)], axis=1)

def layer_norm(value):
    center = value - lax.optimization_barrier(jnp.mean(value, axis=1, keepdims=True))
    return center * lax.rsqrt(lax.optimization_barrier(jnp.mean(center * center, axis=1, keepdims=True)) + 1e-06)

def group_forward(params, tokens, label, times, segments):
    ada_weight, ada_bias, qkv_weight, qv_bias, proj_weight, proj_bias, up_weight, up_bias, down_weight, down_bias = params
    cond = label + time_embed(times, D)
    modul = low_back(product(low(jax.nn.silu(cond)), ada_weight) + ada_bias)
    onehot = (segments[:, None] == jnp.arange(IMG_GRP, dtype=jnp.int32)[None, :]).astype(jnp.float32)
    per_token = product(onehot, modul)
    shift_a, scale_a, gate_a, shift_m, scale_m, gate_m = jnp.split(per_token, 6, axis=1)
    attn_in = low(layer_norm(tokens) * (1.0 + scale_a) + shift_a)
    qkv_bias = jnp.concatenate([qv_bias[:D], jnp.zeros((D,), jnp.float32), qv_bias[D:]])
    qkv = low(low_back(product(attn_in, qkv_weight) + qkv_bias))
    same = segments[:, None] == segments[None, :]
    score_scale = 1.0 / math.sqrt(HEAD_DIM)

    def split_heads(matrix):
        return matrix.reshape(GROUP_TOK, HEADS, HEAD_DIM).transpose(1, 0, 2)

    def one_head(operands):
        query, keys, values = operands
        scores = product(query, keys.T) * score_scale
        scores = low_back(jnp.where(same, scores, -1e+30))
        probs = jax.nn.softmax(scores, axis=1)
        return product(low(probs), values)
    heads = lax.map(jax.checkpoint(one_head), (split_heads(qkv[:, :D]), split_heads(qkv[:, D:2 * D]), split_heads(qkv[:, 2 * D:])))
    heads = low(low_back(heads.transpose(1, 0, 2).reshape(GROUP_TOK, D)))
    attn_out = low_back(product(heads, proj_weight) + proj_bias)
    middle = tokens + gate_a * attn_out
    mlp_in = low(layer_norm(middle) * (1.0 + scale_m) + shift_m)
    pre_act = low_back(product(mlp_in, up_weight) + up_bias)
    act_low = low(jax.nn.gelu(pre_act, approximate=True))
    mlp_out = low_back(product(act_low, down_weight) + down_bias)
    return middle + gate_m * mlp_out

def reference(block_input, label_embed, time_index, segment_ids, ada_weight, ada_bias, qkv_weight, qv_bias, proj_weight, proj_bias, up_weight, up_bias, down_weight, down_bias, bin_weight, out_cotangent):
    params = tuple((value.astype(jnp.float32) for value in (ada_weight, ada_bias, qkv_weight, qv_bias, proj_weight, proj_bias, up_weight, up_bias, down_weight, down_bias)))
    tokens = block_input.astype(jnp.float32).reshape(BINS, GROUP_TOK, D)
    labels = label_embed.reshape(BINS, IMG_GRP, D)
    times = time_index.reshape(BINS, IMG_GRP)
    segments = segment_ids.reshape(BINS, GROUP_TOK)

    def forward(params, tokens, labels):

        def one_group(operands):
            return group_forward(params, *operands)
        return lax.map(jax.checkpoint(one_group), (tokens, labels, times, segments))
    output, back_fn = jax.vjp(forward, params, tokens, labels)
    weighted = out_cotangent.astype(jnp.float32).reshape(BINS, GROUP_TOK, D) * bin_weight[:, None, None]
    grad_params, grad_tokens, grad_labels = back_fn(weighted)
    return (output.reshape(TOKENS, D), grad_tokens.reshape(TOKENS, D), grad_labels.reshape(IMAGES, D), grad_params[0], grad_params[1], grad_params[2], grad_params[3], grad_params[4], grad_params[5], grad_params[6], grad_params[7], grad_params[8], grad_params[9])
```

```python
import functools
import math

import jax
import jax.numpy as jnp
from jax import lax
from jax.experimental import pallas as pl
from jax.experimental.pallas import tpu as pltpu
from jax.sharding import PartitionSpec as P

HEADS = 16
HEAD_DIM = 72
UNIT = 256
LOG2E = 1.0 / math.log(2.0)
SCALE2 = LOG2E / math.sqrt(HEAD_DIM)
WIN = 256


def dot_nt(a, b):
    return lax.dot_general(a, b, (((1,), (1,)), ((), ())), preferred_element_type=jnp.float32)


def dot_nn(a, b):
    return lax.dot_general(a, b, (((1,), (0,)), ((), ())), preferred_element_type=jnp.float32)


def dot_tn(a, b):
    return lax.dot_general(a, b, (((0,), (0,)), ((), ())), preferred_element_type=jnp.float32)


def head_window(head, width):
    first = jnp.minimum(lax.div(head * HEAD_DIM, 128), width // 128 - 2)
    return pl.multiple_of(first * 128, 128)


def head_mask(head, base, rows):
    lane = lax.broadcasted_iota(jnp.int32, (rows, WIN), 1) + base
    return (lane >= head * HEAD_DIM) & (lane < (head + 1) * HEAD_DIM)


def attend_kernel(meta, q, k, v, kh, vh, out, lse):
    width = q.shape[1]
    lse[...] = jnp.zeros_like(lse)

    def one_head(head, carry):
        base = head_window(head, width)
        win = pl.ds(base, WIN)

        def attend(row, count, parts):
            rows = pl.ds(row, count)
            mask = head_mask(head, base, count)
            query = jnp.where(mask, q[rows, win], jnp.zeros((), jnp.bfloat16))
            scores = [dot_nt(query, kr[pl.ds(at, n), win]) for kr, vr, at, n in parts]
            top = functools.reduce(
                jnp.maximum, [jnp.max(s, axis=1, keepdims=True) for s in scores]
            )
            expo = [jnp.exp2((s - top) * SCALE2) for s in scores]
            total = sum(jnp.sum(e, axis=1, keepdims=True) for e in expo)
            summed = sum(
                dot_nn(e.astype(jnp.bfloat16), vr[pl.ds(at, n), win])
                for e, (kr, vr, at, n) in zip(expo, parts)
            )
            value = (summed / total).astype(jnp.bfloat16)
            out[rows, win] = jnp.where(mask, value, out[rows, win])
            lane = lax.broadcasted_iota(jnp.int32, (count, 128), 1)
            lse[rows, :] = jnp.where(lane == head, top * SCALE2 + jnp.log2(total), lse[rows, :])

        def alone(row):
            attend(row, UNIT, [(k, v, row, UNIT)])

        @pl.when(meta[0] == 0)
        def _():
            alone(0)
            alone(UNIT)

        @pl.when(meta[0] == 1)
        def _():
            own = pl.multiple_of(meta[1] * UNIT, UNIT)
            other = pl.multiple_of(UNIT - meta[1] * UNIT, UNIT)
            attend(own, UNIT, [(k, v, own, UNIT), (kh, vh, 0, 3 * UNIT)])
            alone(other)

        @pl.when(meta[0] == 2)
        def _():
            attend(0, UNIT, [(k, v, 0, 2 * UNIT), (kh, vh, 0, 2 * UNIT)])
            attend(UNIT, UNIT, [(k, v, 0, 2 * UNIT), (kh, vh, 0, 2 * UNIT)])

        return carry

    lax.fori_loop(0, HEADS, one_head, 0)


def attend(meta, q, k, v, kh, vh):
    rows, width = q.shape
    return pl.pallas_call(
        attend_kernel,
        out_shape=(
            jax.ShapeDtypeStruct((rows, width), jnp.bfloat16),
            jax.ShapeDtypeStruct((rows, 128), jnp.float32),
        ),
        in_specs=[pl.BlockSpec(memory_space=pltpu.SMEM)]
        + [pl.BlockSpec(memory_space=pltpu.VMEM)] * 5,
        out_specs=[pl.BlockSpec(memory_space=pltpu.VMEM)] * 2,
        compiler_params=pltpu.CompilerParams(vmem_limit_bytes=48 << 20),
        cost_estimate=pl.CostEstimate(
            flops=16 * 2 * 2 * 512 * 1024 * 256, bytes_accessed=10 << 20, transcendentals=16 * 512 * 1024
        ),
        name="attend",
    )(meta, q, k, v, kh, vh)


def own_back_kernel(meta, q, g, stats, k, v, kh, vh, grad_q, grad_k, grad_v):
    width = q.shape[1]
    grad_q[...] = jnp.zeros_like(grad_q)
    grad_k[...] = jnp.zeros_like(grad_k)
    grad_v[...] = jnp.zeros_like(grad_v)
    scale = 1.0 / math.sqrt(HEAD_DIM)

    def one_head(head, carry):
        base = head_window(head, width)
        win = pl.ds(base, WIN)

        def back(row, count, parts):
            rows = pl.ds(row, count)
            mask = head_mask(head, base, count)
            zero = jnp.zeros((), jnp.bfloat16)
            query = jnp.where(mask, q[rows, win], zero)
            grad = jnp.where(mask, g[rows, win], zero)
            lse = stats[pl.ds(head, 1), rows]
            delta = stats[pl.ds(head + HEADS, 1), rows]
            total = jnp.zeros((count, WIN), jnp.float32)
            for kr, vr, at, n, own in parts:
                keys = kr[pl.ds(at, n), win]
                probs = jnp.exp2(dot_nt(keys, query) * SCALE2 - lse)
                grad_probs = dot_nt(vr[pl.ds(at, n), win], grad)
                grad_scores = (probs * (grad_probs - delta)).astype(jnp.bfloat16)
                total += dot_tn(grad_scores, keys)
                if own:
                    grad_k[pl.ds(at, n), win] += dot_nn(grad_scores, query)
                    grad_v[pl.ds(at, n), win] += dot_nn(probs.astype(jnp.bfloat16), grad)
            grad_q[rows, win] = jnp.where(
                mask, (total * scale).astype(jnp.bfloat16), grad_q[rows, win]
            )

        def alone(row):
            back(row, UNIT, [(k, v, row, UNIT, True)])

        @pl.when(meta[0] == 0)
        def _():
            alone(0)
            alone(UNIT)

        @pl.when(meta[0] == 1)
        def _():
            own = pl.multiple_of(meta[1] * UNIT, UNIT)
            other = pl.multiple_of(UNIT - meta[1] * UNIT, UNIT)
            back(own, UNIT, [(k, v, own, UNIT, True), (kh, vh, 0, 3 * UNIT, False)])
            alone(other)

        @pl.when(meta[0] == 2)
        def _():
            back(0, 2 * UNIT, [(k, v, 0, 2 * UNIT, True), (kh, vh, 0, 2 * UNIT, False)])

        return carry

    lax.fori_loop(0, HEADS, one_head, 0)


def own_back(meta, q, g, stats, k, v, kh, vh):
    rows, width = q.shape
    return pl.pallas_call(
        own_back_kernel,
        out_shape=(
            jax.ShapeDtypeStruct((rows, width), jnp.bfloat16),
            jax.ShapeDtypeStruct((rows, width), jnp.float32),
            jax.ShapeDtypeStruct((rows, width), jnp.float32),
        ),
        in_specs=[pl.BlockSpec(memory_space=pltpu.SMEM)]
        + [pl.BlockSpec(memory_space=pltpu.VMEM)] * 7,
        out_specs=[pl.BlockSpec(memory_space=pltpu.VMEM)] * 3,
        compiler_params=pltpu.CompilerParams(vmem_limit_bytes=56 << 20),
        cost_estimate=pl.CostEstimate(
            flops=16 * 2 * 4 * 512 * 1024 * 256, bytes_accessed=20 << 20, transcendentals=16 * 512 * 1024
        ),
        name="own_back",
    )(meta, q, g, stats, k, v, kh, vh)


def halo_back_kernel(meta, qh, gh, stats, k, v, part_k, part_v, grad_k, grad_v, acc_k, acc_v):
    width = k.shape[1]
    acc_k[...] = part_k[...]
    acc_v[...] = part_v[...]
    scale = 1.0 / math.sqrt(HEAD_DIM)

    def one_head(head, carry):
        base = head_window(head, width)
        win = pl.ds(base, WIN)

        def back(count, row, own_count):
            mask = head_mask(head, base, count)
            zero = jnp.zeros((), jnp.bfloat16)
            query = jnp.where(mask, qh[0:count, win], zero)
            grad = jnp.where(mask, gh[0:count, win], zero)
            lse = stats[pl.ds(head, 1), 0:count]
            delta = stats[pl.ds(head + HEADS, 1), 0:count]
            own = pl.ds(row, own_count)
            probs = jnp.exp2(dot_nt(k[own, win], query) * SCALE2 - lse)
            grad_probs = dot_nt(v[own, win], grad)
            grad_scores = (probs * (grad_probs - delta)).astype(jnp.bfloat16)
            acc_k[own, win] += dot_nn(grad_scores, query)
            acc_v[own, win] += dot_nn(probs.astype(jnp.bfloat16), grad)

        @pl.when(meta[0] == 1)
        def _():
            back(3 * UNIT, pl.multiple_of(meta[1] * UNIT, UNIT), UNIT)

        @pl.when(meta[0] == 2)
        def _():
            back(2 * UNIT, 0, 2 * UNIT)

        return carry

    @pl.when(meta[0] != 0)
    def _():
        lax.fori_loop(0, HEADS, one_head, 0)

    grad_k[...] = (acc_k[...] * scale).astype(jnp.bfloat16)
    grad_v[...] = acc_v[...].astype(jnp.bfloat16)


def halo_back(meta, qh, gh, stats, k, v, part_k, part_v):
    rows, width = k.shape
    return pl.pallas_call(
        halo_back_kernel,
        out_shape=(
            jax.ShapeDtypeStruct((rows, width), jnp.bfloat16),
            jax.ShapeDtypeStruct((rows, width), jnp.bfloat16),
        ),
        in_specs=[pl.BlockSpec(memory_space=pltpu.SMEM)]
        + [pl.BlockSpec(memory_space=pltpu.VMEM)] * 7,
        out_specs=[pl.BlockSpec(memory_space=pltpu.VMEM)] * 2,
        scratch_shapes=[pltpu.VMEM((rows, width), jnp.float32)] * 2,
        compiler_params=pltpu.CompilerParams(vmem_limit_bytes=56 << 20),
        cost_estimate=pl.CostEstimate(
            flops=16 * 2 * 4 * 512 * 512 * 256, bytes_accessed=20 << 20, transcendentals=16 * 512 * 512
        ),
        name="halo_back",
    )(meta, qh, gh, stats, k, v, part_k, part_v)


def time_embed(time_index, width):
    half_width = width // 2
    freqs = jnp.exp(-math.log(10000.0) * jnp.arange(half_width, dtype=jnp.float32) / half_width)
    angles = time_index.astype(jnp.float32)[:, None] * freqs[None, :]
    return jnp.concatenate([jnp.cos(angles), jnp.sin(angles)], axis=1)


def layer_norm(value):
    center = value - jnp.mean(value, axis=-1, keepdims=True)
    inverse = lax.rsqrt(jnp.mean(center * center, axis=-1, keepdims=True) + 1e-06)
    return (center * inverse, inverse)


def norm_back(normed, inverse, grad_normed):
    mean_grad = jnp.mean(grad_normed, axis=-1, keepdims=True)
    mean_cross = jnp.mean(grad_normed * normed, axis=-1, keepdims=True)
    return inverse * (grad_normed - mean_grad - normed * mean_cross)


def flat(value):
    return value.reshape(-1, value.shape[-1])


def by_unit(value):
    return value.reshape(-1, UNIT, value.shape[-1])


def chain(count, step):
    pairs = [(at, at + 1) for at in range(count - 1)]
    return pairs if step > 0 else [(b, a) for a, b in pairs]


def halo_candidates(own, shards):
    up, down = chain(shards, 1), chain(shards, -1)
    left = lax.ppermute(own, "shard", up)
    right = lax.ppermute(own, "shard", down)
    left_far = lax.ppermute(left[UNIT:], "shard", up)
    right_far = lax.ppermute(right[:UNIT], "shard", down)
    return jnp.concatenate([left_far, left, right, right_far], axis=0)


def image_layout(unit_segments, shard):
    units = unit_segments.shape[0]
    first = 2 * shard
    own = lax.dynamic_slice_in_dim(unit_segments, first, 2)
    same = unit_segments[None, :] == own[:, None]
    long = jnp.sum(same, axis=1) > 1
    before = jnp.sum(same[0] & (jnp.arange(units) < first))
    both = long[0] & (own[0] == own[1])
    mode = jnp.where(both, 2, jnp.where(long[0] | long[1], 1, 0))
    which = jnp.where(long[1], 1, 0)
    start = jnp.where(both, 3 - before, jnp.where(long[1], 3, 0))
    slot = start + jnp.arange(3)
    halo_units = jnp.clip(first - 3 + slot + jnp.where(slot >= 3, 2, 0), 0, units - 1)
    meta = jnp.stack([mode, which]).astype(jnp.int32)
    return (meta, start, own, unit_segments[halo_units])


def matmul(left, right):
    return jnp.dot(left, right, preferred_element_type=jnp.float32)


def contract_rows(left, right):
    return lax.dot_general(
        left, right, (((0,), (0,)), ((), ())), preferred_element_type=jnp.float32
    )


def contract_cols(left, right):
    return lax.dot_general(
        left, right, (((1,), (1,)), ((), ())), preferred_element_type=jnp.float32
    )


def gather_weight(local):
    wide = lax.all_gather(local, "shard", axis=1, tiled=True)
    return lax.all_gather(wide, "bin", axis=0, tiled=True)


def reduce_grad(grad):
    short = lax.psum_scatter(grad, "bin", scatter_dimension=0, tiled=True)
    return lax.psum_scatter(short, "shard", scatter_dimension=1, tiled=True).astype(jnp.float32)


def split_low(value):
    high = value.astype(jnp.bfloat16)
    return [high, (value - high.astype(jnp.float32)).astype(jnp.bfloat16)]


def per_device(
    block_input,
    label_embed,
    time_index,
    segment_ids,
    ada_weight,
    ada_bias,
    qkv_weight,
    qv_bias,
    proj_weight,
    proj_bias,
    up_weight,
    up_bias,
    down_weight,
    down_bias,
    bin_weight,
    out_cotangent,
):
    rows, width = block_input.shape
    slots = label_embed.shape[0]
    shards = lax.axis_size("shard")
    shard = lax.axis_index("shard")
    unit_segments = segment_ids.reshape(-1, UNIT)[:, 0]
    meta, halo_start, own_segments, halo_segments = image_layout(unit_segments, shard)
    candidates = halo_candidates(block_input, shards)
    halo_input = lax.dynamic_slice_in_dim(candidates, halo_start * UNIT, 3 * UNIT)

    qkv_full = gather_weight(qkv_weight)
    proj_full = gather_weight(proj_weight)
    up_full = gather_weight(up_weight)
    down_full = gather_weight(down_weight)

    cond = label_embed + time_embed(time_index, width)
    cond_low = jax.nn.silu(cond).astype(jnp.bfloat16)
    cond_all = lax.all_gather(cond_low, "bin", axis=0, tiled=True)
    modul = matmul(cond_low, ada_weight) + ada_bias
    own_mod = modul[own_segments].reshape(-1, 1, 6 * width)
    shift_a, scale_a, gate_a, shift_m, scale_m, gate_m = jnp.split(own_mod, 6, axis=2)
    halo_mod = modul[halo_segments][:, None, : 2 * width]

    tokens = by_unit(block_input.astype(jnp.float32))
    normed, inverse = layer_norm(tokens)
    attn_in = flat((normed * (1.0 + scale_a) + shift_a).astype(jnp.bfloat16))
    halo_normed = layer_norm(by_unit(halo_input.astype(jnp.float32)))[0]
    halo_in = flat(
        (halo_normed * (1.0 + halo_mod[:, :, width:]) + halo_mod[:, :, :width]).astype(jnp.bfloat16)
    )
    qkv_bias = jnp.concatenate([qv_bias[:width], jnp.zeros((width,), jnp.float32), qv_bias[width:]])
    qkv_low = (matmul(attn_in, qkv_full) + qkv_bias).astype(jnp.bfloat16)
    halo_low = (matmul(halo_in, qkv_full) + qkv_bias).astype(jnp.bfloat16)
    query, keys, values = jnp.split(qkv_low, 3, axis=1)
    halo_query, halo_keys, halo_values = jnp.split(halo_low, 3, axis=1)

    heads_low, log_total = attend(meta, query, keys, values, halo_keys, halo_values)
    attn_out = by_unit(matmul(heads_low, proj_full) + proj_bias)
    middle = tokens + gate_a * attn_out
    normed_mlp, inverse_mlp = layer_norm(middle)
    mlp_in = flat((normed_mlp * (1.0 + scale_m) + shift_m).astype(jnp.bfloat16))
    pre_act = matmul(mlp_in, up_full) + up_bias
    act_low = jax.nn.gelu(pre_act, approximate=True).astype(jnp.bfloat16)
    mlp_out = by_unit(matmul(act_low, down_full) + down_bias)
    result = flat(middle + gate_m * mlp_out)

    grad_out = by_unit(out_cotangent.astype(jnp.float32) * bin_weight[0])
    grad_mlp = flat((grad_out * gate_m).astype(jnp.bfloat16))
    grad_down_w = reduce_grad(contract_rows(act_low, grad_mlp).astype(jnp.bfloat16))
    grad_down_b = jnp.sum(grad_mlp.astype(jnp.float32), axis=0)
    grad_act = contract_cols(grad_mlp, down_full)
    gelu_back = jax.vjp(lambda value: jax.nn.gelu(value, approximate=True), pre_act)[1]
    grad_pre = gelu_back(grad_act)[0].astype(jnp.bfloat16)
    grad_up_w = reduce_grad(contract_rows(mlp_in, grad_pre).astype(jnp.bfloat16))
    grad_up_b = jnp.sum(grad_pre.astype(jnp.float32), axis=0)
    grad_in_mlp = by_unit(contract_cols(grad_pre, up_full))
    grad_mid = grad_out + norm_back(normed_mlp, inverse_mlp, grad_in_mlp * (1.0 + scale_m))
    grad_attn = flat((grad_mid * gate_a).astype(jnp.bfloat16))
    grad_proj_w = reduce_grad(contract_rows(heads_low, grad_attn).astype(jnp.bfloat16))
    grad_proj_b = jnp.sum(grad_attn.astype(jnp.float32), axis=0)
    grad_heads = contract_cols(grad_attn, proj_full).astype(jnp.bfloat16)

    own_head = jnp.arange(width)[:, None] // HEAD_DIM == jnp.arange(HEADS)[None, :]
    delta = jnp.dot(
        grad_heads.astype(jnp.float32) * heads_low.astype(jnp.float32),
        own_head.astype(jnp.float32),
        precision=lax.Precision.HIGHEST,
        preferred_element_type=jnp.float32,
    )
    own_stats = jnp.concatenate([log_total[:, :HEADS], delta], axis=1)
    spare = jnp.zeros((rows, 128 - 4 * HEADS), jnp.bfloat16)
    payload = jnp.concatenate([grad_heads] + split_low(own_stats) + [spare], axis=1)
    payload_all = halo_candidates(payload, shards)
    halo_payload = lax.dynamic_slice_in_dim(payload_all, halo_start * UNIT, 3 * UNIT)
    halo_stats = halo_payload[:, width : width + 2 * HEADS].astype(jnp.float32) + halo_payload[
        :, width + 2 * HEADS : width + 4 * HEADS
    ].astype(jnp.float32)
    grad_query, part_keys, part_values = own_back(
        meta, query, grad_heads, own_stats.T, keys, values, halo_keys, halo_values
    )
    grad_keys, grad_values = halo_back(
        meta,
        halo_query,
        halo_payload[:, :width],
        halo_stats.T,
        keys,
        values,
        part_keys,
        part_values,
    )
    grad_qkv = jnp.concatenate([grad_query, grad_keys, grad_values], axis=1)
    grad_qkv_w = reduce_grad(contract_rows(attn_in, grad_qkv).astype(jnp.bfloat16))
    grad_qv_b = jnp.concatenate(
        [
            jnp.sum(grad_query.astype(jnp.float32), axis=0),
            jnp.sum(grad_values.astype(jnp.float32), axis=0),
        ]
    )
    grad_in_attn = by_unit(contract_cols(grad_qkv, qkv_full))
    grad_input = flat(grad_mid + norm_back(normed, inverse, grad_in_attn * (1.0 + scale_a)))

    unit_mod = jnp.concatenate(
        [
            jnp.sum(value, axis=1)
            for value in (
                grad_in_attn,
                grad_in_attn * normed,
                grad_mid * attn_out,
                grad_in_mlp,
                grad_in_mlp * normed_mlp,
                grad_out * mlp_out,
            )
        ],
        axis=1,
    )
    picked = own_segments[:, None] == jnp.arange(slots)[None, :]
    mod_part = jnp.sum(jnp.where(picked[:, :, None], unit_mod[:, None, :], 0.0), axis=0)
    grad_mod = lax.psum(mod_part.astype(jnp.bfloat16), "shard")
    grad_cond_act = contract_cols(grad_mod, ada_weight)
    grad_label = jax.vjp(jax.nn.silu, cond)[1](grad_cond_act)[0]

    bins = lax.axis_size("bin")
    own_width = grad_mod.shape[1] // (bins * shards)
    mod_view = grad_mod.reshape(slots, bins, shards, own_width)
    mod_columns = lax.dynamic_index_in_dim(mod_view, shard, axis=2, keepdims=False)
    mod_columns = lax.all_to_all(mod_columns, "bin", split_axis=1, concat_axis=0, tiled=True)[:, 0]
    grad_ada_w = contract_rows(cond_all, mod_columns)
    grad_ada_b = jnp.sum(mod_columns.astype(jnp.float32), axis=0)

    early = lax.psum(
        jnp.concatenate([grad_proj_b, grad_up_b, grad_down_b]), ("bin", "shard")
    )
    grad_qv_b = lax.psum(grad_qv_b, ("bin", "shard"))
    hidden = up_bias.shape[0]
    return (
        result,
        grad_input,
        grad_label,
        grad_ada_w,
        grad_ada_b,
        grad_qkv_w,
        grad_qv_b,
        grad_proj_w,
        early[:width],
        grad_up_w,
        early[width : width + hidden],
        grad_down_w,
        early[width + hidden :],
    )


def solution(mesh):
    placed = (
        P(("bin", "shard"), None),
        P("bin", None),
        P("bin"),
        P("bin"),
        P(),
        P(),
        P("bin", "shard"),
        P(),
        P("bin", "shard"),
        P(),
        P("bin", "shard"),
        P(),
        P("bin", "shard"),
        P(),
        P("bin"),
        P(("bin", "shard"), None),
    )
    return jax.shard_map(
        per_device,
        mesh=mesh,
        in_specs=placed,
        out_specs=(
            P(("bin", "shard"), None),
            P(("bin", "shard"), None),
            P("bin", None),
            P(None, ("bin", "shard")),
            P(("bin", "shard")),
            P("bin", "shard"),
            P(),
            P("bin", "shard"),
            P(),
            P("bin", "shard"),
            P(),
            P("bin", "shard"),
            P(),
        ),
        check_vma=False,
    )
```

```python
import functools
import math

import jax
import jax.numpy as jnp
from jax import lax
from jax.experimental import pallas as pl
from jax.experimental.pallas import tpu as pltpu
from jax.sharding import PartitionSpec as P

HEADS = 16
HEAD_DIM = 72
UNIT = 256
LOG2E = 1.0 / math.log(2.0)
SCALE2 = LOG2E / math.sqrt(HEAD_DIM)
WIN = 256


def dot_nt(a, b):
    return lax.dot_general(a, b, (((1,), (1,)), ((), ())), preferred_element_type=jnp.float32)


def dot_nn(a, b):
    return lax.dot_general(a, b, (((1,), (0,)), ((), ())), preferred_element_type=jnp.float32)


def dot_tn(a, b):
    return lax.dot_general(a, b, (((0,), (0,)), ((), ())), preferred_element_type=jnp.float32)


def head_window(head, width):
    first = jnp.minimum(lax.div(head * HEAD_DIM, 128), width // 128 - 2)
    return pl.multiple_of(first * 128, 128)


def head_mask(head, base, rows):
    lane = lax.broadcasted_iota(jnp.int32, (rows, WIN), 1) + base
    return (lane >= head * HEAD_DIM) & (lane < (head + 1) * HEAD_DIM)


def attend_kernel(meta, own, halo, out, lse):
    width = out.shape[1]
    lse[...] = jnp.zeros_like(lse)

    def one_head(head):
        base = head_window(head, width)
        win = pl.ds(base, WIN)
        key_win = pl.ds(pl.multiple_of(base + width, 128), WIN)
        value_win = pl.ds(pl.multiple_of(base + 2 * width, 128), WIN)

        def attend(row, count, parts):
            rows = pl.ds(row, count)
            mask = head_mask(head, base, count)
            query = jnp.where(mask, own[rows, win], jnp.zeros((), jnp.bfloat16))
            scores = [dot_nt(query, ref[pl.ds(at, n), key_win]) for ref, at, n in parts]
            top = functools.reduce(
                jnp.maximum, [jnp.max(s, axis=1, keepdims=True) for s in scores]
            )
            expo = [jnp.exp2((s - top) * SCALE2) for s in scores]
            total = sum(jnp.sum(e, axis=1, keepdims=True) for e in expo)
            summed = sum(
                dot_nn(e.astype(jnp.bfloat16), ref[pl.ds(at, n), value_win])
                for e, (ref, at, n) in zip(expo, parts)
            )
            value = (summed / total).astype(jnp.bfloat16)
            out[rows, win] = jnp.where(mask, value, out[rows, win])
            lane = lax.broadcasted_iota(jnp.int32, (count, 128), 1)
            here = (lane == head) | (lane == head + 2 * HEADS)
            lse[rows, :] = jnp.where(here, top * SCALE2 + jnp.log2(total), lse[rows, :])

        return attend

    def alone(attend, row):
        attend(row, UNIT, [(own, row, UNIT)])

    @pl.when(meta[0] == 0)
    def _():
        @pl.loop(0, HEADS, unroll=4)
        def _(head):
            alone(one_head(head), 0)
            alone(one_head(head), UNIT)

    @pl.when(meta[0] == 1)
    def _():
        first = pl.multiple_of(meta[1] * UNIT, UNIT)
        other = pl.multiple_of(UNIT - meta[1] * UNIT, UNIT)

        @pl.loop(0, HEADS, unroll=4)
        def _(head):
            attend = one_head(head)
            attend(first, UNIT, [(own, first, UNIT), (halo, 0, 3 * UNIT)])
            alone(attend, other)

    @pl.when(meta[0] == 2)
    def _():
        @pl.loop(0, HEADS, unroll=4)
        def _(head):
            attend = one_head(head)
            attend(0, UNIT, [(own, 0, 2 * UNIT), (halo, 0, 2 * UNIT)])
            attend(UNIT, UNIT, [(own, 0, 2 * UNIT), (halo, 0, 2 * UNIT)])


def attend(meta, own, halo):
    rows, width = own.shape[0], own.shape[1] // 3
    return pl.pallas_call(
        attend_kernel,
        out_shape=(
            jax.ShapeDtypeStruct((rows, width), jnp.bfloat16),
            jax.ShapeDtypeStruct((rows, 128), jnp.float32),
        ),
        in_specs=[pl.BlockSpec(memory_space=pltpu.SMEM)]
        + [pl.BlockSpec(memory_space=pltpu.VMEM)] * 2,
        out_specs=[pl.BlockSpec(memory_space=pltpu.VMEM)] * 2,
        compiler_params=pltpu.CompilerParams(vmem_limit_bytes=48 << 20),
        cost_estimate=pl.CostEstimate(
            flops=2 * 2 * 512 * 1024 * WIN * HEADS,
            bytes_accessed=10 << 20,
            transcendentals=HEADS * 512 * 1024,
        ),
        name="attend",
    )(meta, own, halo)


def own_back_kernel(meta, own, halo, g, stats, grad_q, grad_k, grad_v, turned):
    width = g.shape[1]
    grad_q[...] = jnp.zeros_like(grad_q)
    grad_k[...] = jnp.zeros_like(grad_k)
    grad_v[...] = jnp.zeros_like(grad_v)
    turned[...] = stats[...].T
    scale = 1.0 / math.sqrt(HEAD_DIM)

    def one_head(head):
        base = head_window(head, width)
        win = pl.ds(base, WIN)
        key_win = pl.ds(pl.multiple_of(base + width, 128), WIN)
        value_win = pl.ds(pl.multiple_of(base + 2 * width, 128), WIN)

        def back(row, count, parts):
            rows = pl.ds(row, count)
            mask = head_mask(head, base, count)
            zero = jnp.zeros((), jnp.bfloat16)
            query = jnp.where(mask, own[rows, win], zero)
            grad = jnp.where(mask, g[rows, win], zero)
            lse = turned[pl.ds(head, 1), rows]
            delta = turned[pl.ds(head + HEADS, 1), rows]
            total = jnp.zeros((count, WIN), jnp.float32)
            for ref, at, n, mine in parts:
                keys = ref[pl.ds(at, n), key_win]
                probs = jnp.exp2(dot_nt(keys, query) * SCALE2 - lse)
                grad_probs = dot_nt(ref[pl.ds(at, n), value_win], grad)
                grad_scores = (probs * (grad_probs - delta)).astype(jnp.bfloat16)
                total += dot_tn(grad_scores, keys)
                if mine:
                    grad_k[pl.ds(at, n), win] += dot_nn(grad_scores, query)
                    grad_v[pl.ds(at, n), win] += dot_nn(probs.astype(jnp.bfloat16), grad)
            grad_q[rows, win] = jnp.where(
                mask, (total * scale).astype(jnp.bfloat16), grad_q[rows, win]
            )

        return back

    def alone(back, row):
        back(row, UNIT, [(own, row, UNIT, True)])

    @pl.when(meta[0] == 0)
    def _():
        @pl.loop(0, HEADS, unroll=4)
        def _(head):
            back = one_head(head)
            alone(back, 0)
            alone(back, UNIT)

    @pl.when(meta[0] == 1)
    def _():
        first = pl.multiple_of(meta[1] * UNIT, UNIT)
        other = pl.multiple_of(UNIT - meta[1] * UNIT, UNIT)

        @pl.loop(0, HEADS, unroll=4)
        def _(head):
            back = one_head(head)
            back(first, UNIT, [(own, first, UNIT, True), (halo, 0, 3 * UNIT, False)])
            alone(back, other)

    @pl.when(meta[0] == 2)
    def _():
        @pl.loop(0, HEADS, unroll=4)
        def _(head):
            back = one_head(head)
            back(0, 2 * UNIT, [(own, 0, 2 * UNIT, True), (halo, 0, 2 * UNIT, False)])


def own_back(meta, own, halo, g, stats):
    rows, width = g.shape
    return pl.pallas_call(
        own_back_kernel,
        out_shape=(
            jax.ShapeDtypeStruct((rows, width), jnp.bfloat16),
            jax.ShapeDtypeStruct((rows, width), jnp.float32),
            jax.ShapeDtypeStruct((rows, width), jnp.float32),
        ),
        in_specs=[pl.BlockSpec(memory_space=pltpu.SMEM)]
        + [pl.BlockSpec(memory_space=pltpu.VMEM)] * 4,
        out_specs=[pl.BlockSpec(memory_space=pltpu.VMEM)] * 3,
        scratch_shapes=[pltpu.VMEM((128, rows), jnp.float32)],
        compiler_params=pltpu.CompilerParams(vmem_limit_bytes=56 << 20),
        cost_estimate=pl.CostEstimate(
            flops=2 * 4 * 512 * 1024 * WIN * HEADS,
            bytes_accessed=20 << 20,
            transcendentals=HEADS * 512 * 1024,
        ),
        name="own_back",
    )(meta, own, halo, g, stats)


def halo_back_kernel(
    meta, own, qh, far_left, left, right, far_right, grad_q, part_k, part_v, out, gh, turned, acc_k, acc_v
):
    width = part_k.shape[1]
    acc_k[...] = part_k[...]
    acc_v[...] = part_v[...]
    scale = 1.0 / math.sqrt(HEAD_DIM)
    units = [(far_left, 0), (left, 0), (left, UNIT), (right, 0), (right, UNIT), (far_right, 0)]

    def one_head(head):
        base = head_window(head, width)
        win = pl.ds(base, WIN)
        key_win = pl.ds(pl.multiple_of(base + width, 128), WIN)
        value_win = pl.ds(pl.multiple_of(base + 2 * width, 128), WIN)

        def back(count, row, own_count):
            mask = head_mask(head, base, count)
            zero = jnp.zeros((), jnp.bfloat16)
            query = jnp.where(mask, qh[0:count, win], zero)
            grad = jnp.where(mask, gh[0:count, win], zero)
            lse = turned[pl.ds(head, 1), 0:count]
            delta = turned[pl.ds(head + HEADS, 1), 0:count]
            rows = pl.ds(row, own_count)
            probs = jnp.exp2(dot_nt(own[rows, key_win], query) * SCALE2 - lse)
            grad_probs = dot_nt(own[rows, value_win], grad)
            grad_scores = (probs * (grad_probs - delta)).astype(jnp.bfloat16)
            acc_k[rows, win] += dot_nn(grad_scores, query)
            acc_v[rows, win] += dot_nn(probs.astype(jnp.bfloat16), grad)

        return back

    @pl.when(meta[0] != 0)
    def _():
        for at in range(3):
            for unit in range(at, at + 4):
                ref, row = units[unit]

                @pl.when(meta[2] + at == unit)
                def _(ref=ref, row=row, at=at):
                    gh[at * UNIT : (at + 1) * UNIT, :] = ref[row : row + UNIT, :]

        tail = gh[:, width:].astype(jnp.float32).T
        turned[...] = tail[: 2 * HEADS] + tail[2 * HEADS : 4 * HEADS]

    @pl.when(meta[0] == 1)
    def _():
        row = pl.multiple_of(meta[1] * UNIT, UNIT)

        @pl.loop(0, HEADS, unroll=4)
        def _(head):
            one_head(head)(3 * UNIT, row, UNIT)

    @pl.when(meta[0] == 2)
    def _():
        @pl.loop(0, HEADS, unroll=4)
        def _(head):
            one_head(head)(2 * UNIT, 0, 2 * UNIT)

    out[:, :width] = grad_q[...]
    out[:, width : 2 * width] = (acc_k[...] * scale).astype(jnp.bfloat16)
    out[:, 2 * width :] = acc_v[...].astype(jnp.bfloat16)


def halo_back(meta, own, halo, pieces, grad_q, part_k, part_v):
    rows, width = part_k.shape
    halo_rows = halo.shape[0]

    def whole(value):
        return pl.BlockSpec(value.shape, lambda step: (0, 0))

    return pl.pallas_call(
        halo_back_kernel,
        grid=(1,),
        out_shape=jax.ShapeDtypeStruct((rows, 3 * width), jnp.bfloat16),
        in_specs=[pl.BlockSpec(memory_space=pltpu.SMEM), whole(own)]
        + [pl.BlockSpec((halo_rows, width), lambda step: (0, 0))]
        + [whole(value) for value in (*pieces, grad_q, part_k, part_v)],
        out_specs=pl.BlockSpec((rows, 3 * width), lambda step: (0, 0)),
        scratch_shapes=[
            pltpu.VMEM((halo_rows, pieces[0].shape[1]), jnp.bfloat16),
            pltpu.VMEM((2 * HEADS, halo_rows), jnp.float32),
        ]
        + [pltpu.VMEM((rows, width), jnp.float32)] * 2,
        compiler_params=pltpu.CompilerParams(vmem_limit_bytes=60 << 20),
        cost_estimate=pl.CostEstimate(
            flops=2 * 4 * 512 * 512 * WIN * HEADS,
            bytes_accessed=20 << 20,
            transcendentals=HEADS * 512 * 512,
        ),
        name="halo_back",
    )(meta, own, halo, *pieces, grad_q, part_k, part_v)


def time_embed(time_index, width):
    half_width = width // 2
    freqs = jnp.exp(-math.log(10000.0) * jnp.arange(half_width, dtype=jnp.float32) / half_width)
    angles = time_index.astype(jnp.float32)[:, None] * freqs[None, :]
    return jnp.concatenate([jnp.cos(angles), jnp.sin(angles)], axis=1)


def layer_norm(value):
    center = value - jnp.mean(value, axis=-1, keepdims=True)
    inverse = lax.rsqrt(jnp.mean(center * center, axis=-1, keepdims=True) + 1e-06)
    return (center * inverse, inverse)


def norm_back(normed, inverse, grad_normed):
    mean_grad = jnp.mean(grad_normed, axis=-1, keepdims=True)
    mean_cross = jnp.mean(grad_normed * normed, axis=-1, keepdims=True)
    return inverse * (grad_normed - mean_grad - normed * mean_cross)


def by_unit(value):
    return value.reshape(-1, UNIT, value.shape[-1])


def per_token(rows):
    units, width = rows.shape
    return jnp.broadcast_to(rows[:, None, :], (units, UNIT, width)).reshape(units * UNIT, width)


def chain(count, step):
    return [(at, at + step) for at in range(count) if 0 <= at + step < count]


def send_halo(own, shards):
    left = lax.ppermute(own, "shard", chain(shards, 1))
    right = lax.ppermute(own, "shard", chain(shards, -1))
    return left, right


def send_far(left, right, shards, step):
    left_far = lax.ppermute(left, "shard", chain(shards, step))
    right_far = lax.ppermute(right, "shard", chain(shards, -step))
    return left_far, right_far


def image_layout(unit_segments, shard):
    units = unit_segments.shape[0]
    first = 2 * shard
    own = lax.dynamic_slice_in_dim(unit_segments, first, 2)
    same = unit_segments[None, :] == own[:, None]
    long = jnp.sum(same, axis=1) > 1
    before = jnp.sum(same[0] & (jnp.arange(units) < first))
    both = long[0] & (own[0] == own[1])
    mode = jnp.where(both, 2, jnp.where(long[0] | long[1], 1, 0))
    which = jnp.where(long[1], 1, 0)
    start = jnp.where(both, 3 - before, jnp.where(long[1], 3, 0))
    slot = start + jnp.arange(3)
    halo_units = jnp.clip(first - 3 + slot + jnp.where(slot >= 3, 2, 0), 0, units - 1)
    meta = jnp.stack([mode, which, start]).astype(jnp.int32)
    return (meta, start, own, unit_segments[halo_units])


def matmul(left, right):
    return jnp.dot(left, right, preferred_element_type=jnp.float32)


def contract_rows(left, right):
    return lax.dot_general(
        left, right, (((0,), (0,)), ((), ())), preferred_element_type=jnp.float32
    )


def contract_cols(left, right):
    return lax.dot_general(
        left, right, (((1,), (1,)), ((), ())), preferred_element_type=jnp.float32
    )


def flipped(mask):
    return [(at, at ^ mask) for at in range(8)]


def swap(value, mask):
    return lax.ppermute(value, "bin", flipped(mask))


def rotate(value, count, step):
    return lax.ppermute(value, "shard", [(at, (at + step) % count) for at in range(count)])


def place_kernel(spots, *refs):
    pieces, out, sems = refs[:-2], refs[-2], refs[-1]
    copies = []
    for at, piece in enumerate(pieces):
        start = pl.multiple_of(spots[at], 16)
        copies.append(
            pltpu.make_async_copy(piece, out.at[pl.ds(start, piece.shape[0])], sems.at[at])
        )
    for copy in copies:
        copy.start()
    for copy in copies:
        copy.wait()


def place_rows(spots, pieces):
    rows = sum(piece.shape[0] for piece in pieces)
    width = pieces[0].shape[1]
    return pl.pallas_call(
        place_kernel,
        out_shape=jax.ShapeDtypeStruct((rows, width), pieces[0].dtype),
        in_specs=[pl.BlockSpec(memory_space=pltpu.SMEM)]
        + [pl.BlockSpec(memory_space=pl.ANY)] * len(pieces),
        out_specs=pl.BlockSpec(memory_space=pl.ANY),
        scratch_shapes=[pltpu.SemaphoreType.DMA((len(pieces),))],
        compiler_params=pltpu.CompilerParams(vmem_limit_bytes=1 << 20),
        cost_estimate=pl.CostEstimate(
            flops=0, bytes_accessed=4 * rows * width, transcendentals=0
        ),
        name="place_rows",
    )(jnp.stack(spots).astype(jnp.int32), *pieces)


def after(value, *others):
    return lax.optimization_barrier((value,) + others)[0]


def together(values, *others):
    return lax.optimization_barrier(tuple(values) + others)[: len(values)]


def rotations(local):
    count = lax.axis_size("shard")
    return [rotate(local, count, step) for step in range(1, count)]


def in_order(local, others):
    count = len(others) + 1
    shard = lax.axis_index("shard")
    ring = jnp.stack(list(others[::-1]) + [local])
    twice = jnp.concatenate([ring, ring])
    return lax.dynamic_slice_in_dim(twice, count - 1 - shard, count)


def columns_of(local, others):
    return in_order(local, others).transpose(1, 0, 2).reshape(local.shape[0], -1)


def row_split(rows):
    return (rows // 2 + 15) // 16 * 16


def place_pieces(pieces, swapped):
    me = lax.axis_index("bin")
    rows = pieces[0].shape[0]
    half = row_split(rows)
    starts = [me, me ^ 2, me ^ 4, me ^ 6, me ^ 6]
    offsets = [0, 0, 0, 0, half]
    spots = [start * rows + offset for start, offset in zip(starts, offsets)]
    spots += [(start ^ 1) * rows + offset for start, offset in zip(starts, offsets)]
    return place_rows(spots, list(pieces) + list(swapped))


def column_parts(short):
    count = lax.axis_size("shard")
    shard = lax.axis_index("shard")
    parts = short.reshape(short.shape[0], count, -1)
    return [
        lax.dynamic_index_in_dim(parts, lax.rem(shard + step, count), 1, keepdims=False)
        for step in range(count)
    ]


def rotate_parts(parts):
    count = len(parts)
    return [rotate(part, count, step) for step, part in enumerate(parts) if step > 0]


def sum_wide(parts):
    return sum(part.astype(jnp.float32) for part in parts)


def scatter_columns(short):
    return lax.psum_scatter(short, "shard", scatter_dimension=1, tiled=True)


def stack_kernel(*refs):
    pieces, out = refs[:-1], refs[-1]
    width = out.shape[1]
    row = 0
    for piece in pieces:
        rows = piece.shape[0]
        for at in range(piece.shape[1] // width):
            out[row : row + rows, :] = piece[:, at * width : (at + 1) * width]
            row += rows


def stack_rows(pieces, width):
    rows = sum(piece.size for piece in pieces) // width
    return pl.pallas_call(
        stack_kernel,
        out_shape=jax.ShapeDtypeStruct((rows, width), pieces[0].dtype),
        in_specs=[pl.BlockSpec(memory_space=pltpu.VMEM)] * len(pieces),
        out_specs=pl.BlockSpec(memory_space=pltpu.VMEM),
        compiler_params=pltpu.CompilerParams(vmem_limit_bytes=8 << 20),
        cost_estimate=pl.CostEstimate(flops=0, bytes_accessed=8 * rows * width, transcendentals=0),
        name="stack_rows",
    )(*pieces)


def add_low(first, second):
    return (first.astype(jnp.float32) + second.astype(jnp.float32)).astype(jnp.bfloat16)


def half_blocks(left):
    me = lax.axis_index("bin")
    turned = lax.optimization_barrier(left.T)
    blocks = turned.reshape(8, turned.shape[0] // 8, -1)
    half = row_split(blocks.shape[1])
    result = []
    for flip in (1, 0):
        own, side, over, cross = [
            lax.dynamic_index_in_dim(blocks, me ^ flip ^ mask, 0, keepdims=False)
            for mask in (0, 2, 4, 6)
        ]
        upper = [part[:half] for part in (own, over, side, cross)]
        lower = [part[half:] for part in (own, side, over, cross)]
        result.append(jnp.concatenate(upper + lower))
    return result


def first_parts(total):
    half = row_split(total.shape[0] // 4)
    rest = total.shape[0] // 4 - half
    return total[2 * half : 4 * half], total[4 * half + 2 * rest :]


def second_parts(total, from_x, from_y):
    half = row_split(total.shape[0] // 4)
    rest = total.shape[0] // 4 - half
    low = 4 * half
    top = total[:half].astype(jnp.float32) + from_x[:half].astype(jnp.float32)
    bottom = total[low : low + rest].astype(jnp.float32) + from_y[:rest].astype(jnp.float32)
    return (
        add_low(total[half : 2 * half], from_x[half:]),
        add_low(total[low + rest : low + 2 * rest], from_y[rest:]),
        top,
        bottom,
    )


def last_rows(top, bottom, upper, lower):
    return jnp.concatenate(
        [top + upper.astype(jnp.float32), bottom + lower.astype(jnp.float32)]
    ).astype(jnp.bfloat16)


def split_low(value):
    high = value.astype(jnp.bfloat16)
    return [high, (value - high.astype(jnp.float32)).astype(jnp.bfloat16)]


def per_device(
    block_input,
    label_embed,
    time_index,
    segment_ids,
    ada_weight,
    ada_bias,
    qkv_weight,
    qv_bias,
    proj_weight,
    proj_bias,
    up_weight,
    up_bias,
    down_weight,
    down_bias,
    bin_weight,
    out_cotangent,
):
    rows, width = block_input.shape
    slots = label_embed.shape[0]
    shards = lax.axis_size("shard")
    bins = lax.axis_size("bin")
    shard = lax.axis_index("shard")
    fast = bins == 8
    unit_segments = segment_ids.reshape(-1, UNIT)[:, 0]
    meta, halo_start, own_segments, halo_segments = image_layout(unit_segments, shard)

    cond = label_embed + time_embed(time_index, width)
    cond_low = jax.nn.silu(cond).astype(jnp.bfloat16)
    modul = matmul(cond_low, ada_weight) + ada_bias
    own_mod = modul[own_segments]
    shift_a, scale_a, gate_a, shift_m, scale_m, gate_m = [
        per_token(part) for part in jnp.split(own_mod, 6, axis=1)
    ]
    halo_mod = modul[halo_segments][:, : 2 * width]
    halo_shift, halo_scale = per_token(halo_mod[:, :width]), per_token(halo_mod[:, width:])

    qkv_parts = rotations(qkv_weight)
    proj_parts = rotations(proj_weight)
    tokens = block_input.astype(jnp.float32)
    normed, inverse = layer_norm(tokens)
    attn_in = (normed * (1.0 + scale_a) + shift_a).astype(jnp.bfloat16)
    qkv_wide = columns_of(qkv_weight, together(qkv_parts, attn_in))
    qkv_full = lax.all_gather(qkv_wide, "bin", axis=0, tiled=True)
    proj_wide = columns_of(proj_weight, together(proj_parts, qkv_wide))
    left, right = send_halo(after(block_input, qkv_wide), shards)
    up_parts = rotations(after(up_weight, qkv_wide))
    if fast:
        proj_x, proj_y = swap(proj_wide, 2), swap(proj_wide, 4)
    else:
        proj_full = lax.all_gather(proj_wide, "bin", axis=0, tiled=True)
    left, right = together((left, right), proj_wide)
    far_left, far_right = together((left[UNIT:], right[:UNIT]))
    up_parts = together(up_parts, far_left, far_right)
    left_far, right_far = send_far(far_left, far_right, shards, 1)
    up_wide = columns_of(up_weight, up_parts)
    up_full = lax.all_gather(up_wide, "bin", axis=0, tiled=True)
    if fast:
        proj_x, proj_y = together((proj_x, proj_y), up_wide)
        half = row_split(proj_wide.shape[0])
        proj_cross = [swap(proj_y[:half], 2), swap(proj_x[half:], 4)]
        proj_core = [swap(piece, 1) for piece in (proj_wide, proj_x, proj_y)]
    qkv_bias = jnp.concatenate([qv_bias[:width], jnp.zeros((width,), jnp.float32), qv_bias[width:]])
    qkv_low = (matmul(after(attn_in, up_wide), qkv_full) + qkv_bias).astype(jnp.bfloat16)
    left_far, right_far = together((left_far, right_far), qkv_low)
    down_parts = rotations(after(down_weight, left_far))
    candidates = jnp.concatenate([left_far, left, right, right_far])
    halo_input = lax.dynamic_slice_in_dim(candidates, halo_start * UNIT, 3 * UNIT)
    halo_normed = layer_norm(halo_input.astype(jnp.float32))[0]
    halo_in = (halo_normed * (1.0 + halo_scale) + halo_shift).astype(jnp.bfloat16)
    halo_low = (matmul(halo_in, qkv_full) + qkv_bias).astype(jnp.bfloat16)
    if fast:
        proj_cross = together(proj_cross, halo_low)
        proj_core += [swap(piece, 1) for piece in proj_cross]
        halo_low = after(halo_low, *proj_cross)
    heads_low, log_total = attend(meta, qkv_low, halo_low)
    down_wide = columns_of(down_weight, together(down_parts, heads_low))
    if fast:
        down_x, down_y = swap(down_wide, 2), swap(down_wide, 4)
        proj_core = together(proj_core, down_wide)
        proj_full = place_pieces([proj_wide, proj_x, proj_y] + list(proj_cross), proj_core)
    else:
        down_full = lax.all_gather(down_wide, "bin", axis=0, tiled=True)
    attn_out = matmul(heads_low, proj_full) + proj_bias
    middle = tokens + gate_a * attn_out
    normed_mlp, inverse_mlp = layer_norm(middle)
    mlp_in = (normed_mlp * (1.0 + scale_m) + shift_m).astype(jnp.bfloat16)
    if fast:
        down_x, down_y = together((down_x, down_y), mlp_in)
        half = row_split(down_wide.shape[0])
        down_cross = together((down_y[:half], down_x[half:]))
        up_full = after(up_full, down_cross[0])
        down_cross = [swap(down_cross[0], 2), swap(down_cross[1], 4)]
        down_core = [swap(piece, 1) for piece in (down_wide, down_x, down_y)]
    pre_act = matmul(mlp_in, up_full) + up_bias
    act_low = lax.optimization_barrier(
        jax.nn.gelu(pre_act, approximate=True).astype(jnp.bfloat16)
    )

    slope = jax.vjp(lambda value: jax.nn.gelu(value, approximate=True), after(pre_act, act_low))[1](
        jnp.ones_like(pre_act)
    )[0]
    slope = lax.optimization_barrier(slope.astype(jnp.bfloat16))

    grad_out = out_cotangent.astype(jnp.float32) * bin_weight[0]
    grad_mlp = (grad_out * gate_m).astype(jnp.bfloat16)
    grad_down = contract_rows(act_low, grad_mlp).astype(jnp.bfloat16)
    if fast:
        down_cross = together(down_cross, grad_down, slope)
        down_core += [swap(piece, 1) for piece in down_cross]
        down_full = place_pieces([down_wide, down_x, down_y] + list(down_cross), down_core)
    grad_mlp = after(grad_mlp, grad_down)
    grad_down = lax.psum_scatter(grad_down, "bin", scatter_dimension=0, tiled=True)
    grad_down_b = jnp.sum(grad_mlp.astype(jnp.float32), axis=0)
    grad_act = contract_cols(grad_mlp, down_full)
    grad_pre = (grad_act * slope.astype(jnp.float32)).astype(jnp.bfloat16)
    grad_up_b = jnp.sum(grad_pre.astype(jnp.float32), axis=0)
    grad_up = contract_rows(mlp_in, grad_pre).astype(jnp.bfloat16)
    grad_in_mlp = contract_cols(after(grad_pre, grad_up), up_full)
    grad_up = lax.psum_scatter(grad_up, "bin", scatter_dimension=0, tiled=True)
    grad_mid = grad_out + norm_back(normed_mlp, inverse_mlp, grad_in_mlp * (1.0 + scale_m))
    grad_attn = (grad_mid * gate_a).astype(jnp.bfloat16)
    grad_proj_b = jnp.sum(grad_attn.astype(jnp.float32), axis=0)
    if fast:
        heads_other, heads_mine = half_blocks(heads_low)
        other_proj = matmul(heads_other, grad_attn).astype(jnp.bfloat16)
        grad_attn = after(grad_attn, other_proj)
        got_proj = swap(other_proj, 1)
    grad_heads = contract_cols(grad_attn, proj_full).astype(jnp.bfloat16)

    lane = jnp.arange(128)[None, :]
    own_head = jnp.arange(width)[:, None] // HEAD_DIM + HEADS == lane % (2 * HEADS)
    own_head &= lane < 4 * HEADS
    delta = jnp.dot(
        grad_heads.astype(jnp.float32) * heads_low.astype(jnp.float32),
        own_head.astype(jnp.float32),
        precision=lax.Precision.HIGHEST,
        preferred_element_type=jnp.float32,
    )
    own_stats = log_total + delta
    high, low = split_low(own_stats)
    payload = jnp.concatenate([grad_heads, jnp.where(lane < 2 * HEADS, high, low)], axis=1)
    left, right = send_halo(payload, shards)
    left_far, right_far = send_far(payload[UNIT:], payload[:UNIT], shards, 2)
    if fast:
        total_proj = matmul(after(heads_mine, payload), grad_attn) + got_proj.astype(jnp.float32)
        total_proj = total_proj.astype(jnp.bfloat16)
        proj_x, proj_y, total_proj = together((*first_parts(total_proj), total_proj))
        grad_heads = after(grad_heads, proj_x, proj_y)
        proj_x, proj_y = swap(proj_x, 2), swap(proj_y, 4)
    else:
        grad_proj = contract_rows(heads_low, grad_attn).astype(jnp.bfloat16)
        grad_proj = lax.psum_scatter(grad_proj, "bin", scatter_dimension=0, tiled=True)
    grad_query, part_keys, part_values = own_back(meta, qkv_low, halo_low, grad_heads, own_stats)
    left, right, left_far, right_far = together((left, right, left_far, right_far), grad_query)
    grad_qkv = halo_back(
        meta,
        qkv_low,
        halo_low,
        (left_far, left, right, right_far),
        grad_query,
        part_keys,
        part_values,
    )
    if fast:
        attn_other, attn_mine = half_blocks(attn_in)
        other_qkv = matmul(attn_other, grad_qkv).astype(jnp.bfloat16)
        got_qkv = swap(other_qkv, 1)
        grad_down_w = scatter_columns(after(grad_down, grad_up, other_qkv))
        grad_in_attn = contract_cols(after(grad_qkv, other_qkv), qkv_full)
        total_qkv = matmul(after(attn_mine, grad_in_attn), grad_qkv) + got_qkv.astype(jnp.float32)
        total_qkv = total_qkv.astype(jnp.bfloat16)
        qkv_x, qkv_y, total_qkv = together((*first_parts(total_qkv), total_qkv))
        qkv_x, qkv_y = swap(qkv_x, 2), swap(qkv_y, 4)
        proj_x, proj_y = together((proj_x, proj_y), total_qkv)
        proj_over, proj_side, *proj_kept = second_parts(total_proj, proj_x, proj_y)
        proj_upper, proj_lower = swap(proj_over, 4), swap(proj_side, 2)
        grad_in_attn = after(grad_in_attn, proj_over, proj_side)
    else:
        total_qkv = contract_rows(attn_in, grad_qkv).astype(jnp.bfloat16)
        grad_in_attn = contract_cols(grad_qkv, qkv_full)
    grad_qv_b = jnp.concatenate(
        [
            jnp.sum(grad_qkv[:, :width].astype(jnp.float32), axis=0),
            jnp.sum(grad_qkv[:, 2 * width :].astype(jnp.float32), axis=0),
        ]
    )
    mlp_out = matmul(after(act_low, grad_in_attn), down_full) + down_bias
    result = middle + gate_m * mlp_out
    if fast:
        grad_in_attn = after(grad_in_attn, mlp_out, grad_down_w)
    grad_input = grad_mid + norm_back(normed, inverse, grad_in_attn * (1.0 + scale_a))

    unit_mod = [
        jnp.sum(by_unit(value), axis=1)
        for value in (
            grad_in_attn,
            grad_in_attn * normed,
            grad_mid * attn_out,
            grad_in_mlp,
            grad_in_mlp * normed_mlp,
            grad_out * mlp_out,
        )
    ]
    biases = [part[None, :] for part in (grad_qv_b, grad_proj_b, grad_up_b, grad_down_b)]
    small = stack_rows(unit_mod + biases, width)
    if fast:
        qkv_x, qkv_y = together((qkv_x, qkv_y), small)
        qkv_over, qkv_side, *qkv_kept = second_parts(total_qkv, qkv_x, qkv_y)
        qkv_over, qkv_side = together((qkv_over, qkv_side))
        small = after(small, qkv_over)
        grad_up_w = scatter_columns(after(grad_up, qkv_over))
        qkv_upper, qkv_lower = swap(qkv_over, 4), swap(qkv_side, 2)
        proj_upper, proj_lower = together((proj_upper, proj_lower), qkv_over)
        grad_proj = last_rows(*proj_kept, proj_upper, proj_lower)
        proj_parts = together(column_parts(grad_proj))
        qkv_upper, qkv_lower = together((qkv_upper, qkv_lower), proj_parts[0])
        grad_qkv_w = last_rows(*qkv_kept, qkv_upper, qkv_lower)
        both_parts = together(
            [
                jnp.concatenate(pair, axis=1)
                for pair in zip(column_parts(grad_qkv_w), proj_parts)
            ]
        )
        both_moved = rotate_parts(both_parts)
        last_sent = both_parts[:1]
        both = sum_wide(list(both_parts[:1]) + both_moved)
        grad_up_w = after(grad_up_w, both)
        grad_qkv_w, grad_proj_w = jnp.split(both, [qkv_weight.shape[1]], axis=1)
    else:
        grad_qkv_w = lax.psum_scatter(total_qkv, "bin", scatter_dimension=0, tiled=True)
        grad_qkv_w, grad_proj_w, grad_up_w, grad_down_w = [
            scatter_columns(part) for part in (grad_qkv_w, grad_proj, grad_up, grad_down)
        ]
        last_sent = []
    moved = together(rotations(small), *last_sent)
    small = in_order(small, moved)
    all_units = small[:, :12].reshape(shards, 6, 2, width).transpose(0, 2, 1, 3)
    all_units = all_units.reshape(2 * shards, 6 * width)
    biases = jnp.sum(small[:, 12:], axis=0).reshape(-1)
    picked = unit_segments[None, :] == jnp.arange(slots)[:, None]
    grad_mod = jnp.sum(jnp.where(picked[:, :, None], all_units[None], 0.0), axis=1)
    grad_mod = grad_mod.astype(jnp.bfloat16)
    own_width = grad_mod.shape[1] // (bins * shards)
    mod_view = grad_mod.reshape(slots, bins, shards, own_width)
    mod_columns = lax.dynamic_index_in_dim(mod_view, shard, axis=2, keepdims=False)
    spread = jnp.concatenate(
        [cond_low] + [part.reshape(slots, -1) for part in split_low(biases)], axis=1
    )
    spread = jnp.broadcast_to(spread[:, None, :], (slots, bins, spread.shape[1]))
    traded = lax.all_to_all(
        jnp.concatenate([mod_columns, spread], axis=2),
        "bin",
        split_axis=1,
        concat_axis=0,
        tiled=True,
    )[:, 0]
    grad_cond_act = contract_cols(after(grad_mod, *last_sent), ada_weight)
    grad_label = jax.vjp(jax.nn.silu, cond)[1](grad_cond_act)[0]
    cond_all = traded[:, own_width : own_width + width]
    grad_ada_w = contract_rows(cond_all, traded[:, :own_width])
    grad_ada_b = jnp.sum(traded[:, :own_width].astype(jnp.float32), axis=0)
    high, lower = jnp.split(traded[:, own_width + width :].astype(jnp.float32), 2, axis=1)
    biases = jnp.sum((high + lower).reshape(bins, -1), axis=0)

    hidden = up_bias.shape[0]
    ends = [2 * width, 3 * width, 3 * width + hidden]
    grad_qv_b, grad_proj_b, grad_up_b, grad_down_b = jnp.split(biases, ends)
    return (
        result,
        grad_input,
        grad_label,
        grad_ada_w,
        grad_ada_b,
        grad_qkv_w.astype(jnp.float32),
        grad_qv_b,
        grad_proj_w.astype(jnp.float32),
        grad_proj_b,
        grad_up_w.astype(jnp.float32),
        grad_up_b,
        grad_down_w.astype(jnp.float32),
        grad_down_b,
    )


def solution(mesh):
    placed = (
        P(("bin", "shard"), None),
        P("bin", None),
        P("bin"),
        P("bin"),
        P(),
        P(),
        P("bin", "shard"),
        P(),
        P("bin", "shard"),
        P(),
        P("bin", "shard"),
        P(),
        P("bin", "shard"),
        P(),
        P("bin"),
        P(("bin", "shard"), None),
    )
    return jax.shard_map(
        per_device,
        mesh=mesh,
        in_specs=placed,
        out_specs=(
            P(("bin", "shard"), None),
            P(("bin", "shard"), None),
            P("bin", None),
            P(None, ("bin", "shard")),
            P(("bin", "shard")),
            P("bin", "shard"),
            P(),
            P("bin", "shard"),
            P(),
            P("bin", "shard"),
            P(),
            P("bin", "shard"),
            P(),
        ),
        check_vma=False,
    )
```

```python
import functools
import math

import jax
import jax.numpy as jnp
from jax import lax
from jax.experimental import pallas as pl
from jax.experimental.pallas import tpu as pltpu
from jax.sharding import PartitionSpec as P

HEADS = 16
HEAD_DIM = 72
UNIT = 256
LOG2E = 1.0 / math.log(2.0)
SCALE2 = LOG2E / math.sqrt(HEAD_DIM)
WIN = 256


def dot_nt(a, b):
    return lax.dot_general(a, b, (((1,), (1,)), ((), ())), preferred_element_type=jnp.float32)


def dot_nn(a, b):
    return lax.dot_general(a, b, (((1,), (0,)), ((), ())), preferred_element_type=jnp.float32)


def dot_tn(a, b):
    return lax.dot_general(a, b, (((0,), (0,)), ((), ())), preferred_element_type=jnp.float32)


def head_window(head, width):
    first = jnp.minimum(lax.div(head * HEAD_DIM, 128), width // 128 - 2)
    return pl.multiple_of(first * 128, 128)


def head_mask(head, base, rows):
    lane = lax.broadcasted_iota(jnp.int32, (rows, WIN), 1) + base
    return (lane >= head * HEAD_DIM) & (lane < (head + 1) * HEAD_DIM)


def attend_kernel(meta, own, halo, out, lse):
    width = out.shape[1]
    lse[...] = jnp.zeros_like(lse)

    def one_head(head):
        base = head_window(head, width)
        win = pl.ds(base, WIN)
        key_win = pl.ds(pl.multiple_of(base + width, 128), WIN)
        value_win = pl.ds(pl.multiple_of(base + 2 * width, 128), WIN)

        def attend(row, count, parts):
            rows = pl.ds(row, count)
            mask = head_mask(head, base, count)
            query = jnp.where(mask, own[rows, win], jnp.zeros((), jnp.bfloat16))
            scores = [dot_nt(query, ref[pl.ds(at, n), key_win]) for ref, at, n in parts]
            top = functools.reduce(
                jnp.maximum, [jnp.max(s, axis=1, keepdims=True) for s in scores]
            )
            expo = [jnp.exp2((s - top) * SCALE2) for s in scores]
            total = sum(jnp.sum(e, axis=1, keepdims=True) for e in expo)
            summed = sum(
                dot_nn(e.astype(jnp.bfloat16), ref[pl.ds(at, n), value_win])
                for e, (ref, at, n) in zip(expo, parts)
            )
            value = (summed / total).astype(jnp.bfloat16)
            out[rows, win] = jnp.where(mask, value, out[rows, win])
            lane = lax.broadcasted_iota(jnp.int32, (count, 128), 1)
            here = (lane == head) | (lane == head + 2 * HEADS)
            lse[rows, :] = jnp.where(here, top * SCALE2 + jnp.log2(total), lse[rows, :])

        return attend

    def alone(attend, row):
        attend(row, UNIT, [(own, row, UNIT)])

    @pl.when(meta[0] == 0)
    def _():
        @pl.loop(0, HEADS, unroll=4)
        def _(head):
            alone(one_head(head), 0)
            alone(one_head(head), UNIT)

    @pl.when(meta[0] == 1)
    def _():
        first = pl.multiple_of(meta[1] * UNIT, UNIT)
        other = pl.multiple_of(UNIT - meta[1] * UNIT, UNIT)

        @pl.loop(0, HEADS, unroll=4)
        def _(head):
            attend = one_head(head)
            attend(first, UNIT, [(own, first, UNIT), (halo, 0, 3 * UNIT)])
            alone(attend, other)

    @pl.when(meta[0] == 2)
    def _():
        @pl.loop(0, HEADS, unroll=4)
        def _(head):
            attend = one_head(head)
            attend(0, UNIT, [(own, 0, 2 * UNIT), (halo, 0, 2 * UNIT)])
            attend(UNIT, UNIT, [(own, 0, 2 * UNIT), (halo, 0, 2 * UNIT)])


def attend(meta, own, halo):
    rows, width = own.shape[0], own.shape[1] // 3
    return pl.pallas_call(
        attend_kernel,
        out_shape=(
            jax.ShapeDtypeStruct((rows, width), jnp.bfloat16),
            jax.ShapeDtypeStruct((rows, 128), jnp.float32),
        ),
        in_specs=[pl.BlockSpec(memory_space=pltpu.SMEM)]
        + [pl.BlockSpec(memory_space=pltpu.VMEM)] * 2,
        out_specs=[pl.BlockSpec(memory_space=pltpu.VMEM)] * 2,
        compiler_params=pltpu.CompilerParams(vmem_limit_bytes=48 << 20),
        cost_estimate=pl.CostEstimate(
            flops=2 * 2 * 512 * 1024 * WIN * HEADS,
            bytes_accessed=10 << 20,
            transcendentals=HEADS * 512 * 1024,
        ),
        name="attend",
    )(meta, own, halo)


def own_back_kernel(meta, own, halo, g, stats, grad_q, grad_k, grad_v, turned):
    width = g.shape[1]
    grad_q[...] = jnp.zeros_like(grad_q)
    grad_k[...] = jnp.zeros_like(grad_k)
    grad_v[...] = jnp.zeros_like(grad_v)
    turned[...] = stats[...].T
    scale = 1.0 / math.sqrt(HEAD_DIM)

    def one_head(head):
        base = head_window(head, width)
        win = pl.ds(base, WIN)
        key_win = pl.ds(pl.multiple_of(base + width, 128), WIN)
        value_win = pl.ds(pl.multiple_of(base + 2 * width, 128), WIN)

        def back(row, count, parts):
            rows = pl.ds(row, count)
            mask = head_mask(head, base, count)
            zero = jnp.zeros((), jnp.bfloat16)
            query = jnp.where(mask, own[rows, win], zero)
            grad = jnp.where(mask, g[rows, win], zero)
            lse = turned[pl.ds(head, 1), rows]
            delta = turned[pl.ds(head + HEADS, 1), rows]
            total = jnp.zeros((count, WIN), jnp.float32)
            for ref, at, n, mine in parts:
                keys = ref[pl.ds(at, n), key_win]
                probs = jnp.exp2(dot_nt(keys, query) * SCALE2 - lse)
                grad_probs = dot_nt(ref[pl.ds(at, n), value_win], grad)
                grad_scores = (probs * (grad_probs - delta)).astype(jnp.bfloat16)
                total += dot_tn(grad_scores, keys)
                if mine:
                    grad_k[pl.ds(at, n), win] += dot_nn(grad_scores, query)
                    grad_v[pl.ds(at, n), win] += dot_nn(probs.astype(jnp.bfloat16), grad)
            grad_q[rows, win] = jnp.where(
                mask, (total * scale).astype(jnp.bfloat16), grad_q[rows, win]
            )

        return back

    def alone(back, row):
        back(row, UNIT, [(own, row, UNIT, True)])

    @pl.when(meta[0] == 0)
    def _():
        @pl.loop(0, HEADS, unroll=4)
        def _(head):
            back = one_head(head)
            alone(back, 0)
            alone(back, UNIT)

    @pl.when(meta[0] == 1)
    def _():
        first = pl.multiple_of(meta[1] * UNIT, UNIT)
        other = pl.multiple_of(UNIT - meta[1] * UNIT, UNIT)

        @pl.loop(0, HEADS, unroll=4)
        def _(head):
            back = one_head(head)
            back(first, UNIT, [(own, first, UNIT, True), (halo, 0, 3 * UNIT, False)])
            alone(back, other)

    @pl.when(meta[0] == 2)
    def _():
        @pl.loop(0, HEADS, unroll=4)
        def _(head):
            back = one_head(head)
            back(0, 2 * UNIT, [(own, 0, 2 * UNIT, True), (halo, 0, 2 * UNIT, False)])


def own_back(meta, own, halo, g, stats):
    rows, width = g.shape
    return pl.pallas_call(
        own_back_kernel,
        out_shape=(
            jax.ShapeDtypeStruct((rows, width), jnp.bfloat16),
            jax.ShapeDtypeStruct((rows, width), jnp.float32),
            jax.ShapeDtypeStruct((rows, width), jnp.float32),
        ),
        in_specs=[pl.BlockSpec(memory_space=pltpu.SMEM)]
        + [pl.BlockSpec(memory_space=pltpu.VMEM)] * 4,
        out_specs=[pl.BlockSpec(memory_space=pltpu.VMEM)] * 3,
        scratch_shapes=[pltpu.VMEM((128, rows), jnp.float32)],
        compiler_params=pltpu.CompilerParams(vmem_limit_bytes=56 << 20),
        cost_estimate=pl.CostEstimate(
            flops=2 * 4 * 512 * 1024 * WIN * HEADS,
            bytes_accessed=20 << 20,
            transcendentals=HEADS * 512 * 1024,
        ),
        name="own_back",
    )(meta, own, halo, g, stats)


def halo_back_kernel(
    meta, own, qh, far_left, left, right, far_right, grad_q, part_k, part_v, out, gh, turned, acc_k, acc_v
):
    width = part_k.shape[1]
    acc_k[...] = part_k[...]
    acc_v[...] = part_v[...]
    scale = 1.0 / math.sqrt(HEAD_DIM)
    units = [(far_left, 0), (left, 0), (left, UNIT), (right, 0), (right, UNIT), (far_right, 0)]

    def one_head(head):
        base = head_window(head, width)
        win = pl.ds(base, WIN)
        key_win = pl.ds(pl.multiple_of(base + width, 128), WIN)
        value_win = pl.ds(pl.multiple_of(base + 2 * width, 128), WIN)

        def back(count, row, own_count):
            mask = head_mask(head, base, count)
            zero = jnp.zeros((), jnp.bfloat16)
            query = jnp.where(mask, qh[0:count, win], zero)
            grad = jnp.where(mask, gh[0:count, win], zero)
            lse = turned[pl.ds(head, 1), 0:count]
            delta = turned[pl.ds(head + HEADS, 1), 0:count]
            rows = pl.ds(row, own_count)
            probs = jnp.exp2(dot_nt(own[rows, key_win], query) * SCALE2 - lse)
            grad_probs = dot_nt(own[rows, value_win], grad)
            grad_scores = (probs * (grad_probs - delta)).astype(jnp.bfloat16)
            acc_k[rows, win] += dot_nn(grad_scores, query)
            acc_v[rows, win] += dot_nn(probs.astype(jnp.bfloat16), grad)

        return back

    @pl.when(meta[0] != 0)
    def _():
        for at in range(3):
            for unit in range(at, at + 4):
                ref, row = units[unit]

                @pl.when(meta[2] + at == unit)
                def _(ref=ref, row=row, at=at):
                    gh[at * UNIT : (at + 1) * UNIT, :] = ref[row : row + UNIT, :]

        tail = gh[:, width:].astype(jnp.float32).T
        turned[...] = tail[: 2 * HEADS] + tail[2 * HEADS : 4 * HEADS]

    @pl.when(meta[0] == 1)
    def _():
        row = pl.multiple_of(meta[1] * UNIT, UNIT)

        @pl.loop(0, HEADS, unroll=4)
        def _(head):
            one_head(head)(3 * UNIT, row, UNIT)

    @pl.when(meta[0] == 2)
    def _():
        @pl.loop(0, HEADS, unroll=4)
        def _(head):
            one_head(head)(2 * UNIT, 0, 2 * UNIT)

    out[:, :width] = grad_q[...]
    out[:, width : 2 * width] = (acc_k[...] * scale).astype(jnp.bfloat16)
    out[:, 2 * width :] = acc_v[...].astype(jnp.bfloat16)


def halo_back(meta, own, halo, pieces, grad_q, part_k, part_v):
    rows, width = part_k.shape
    halo_rows = halo.shape[0]

    def whole(value):
        return pl.BlockSpec(value.shape, lambda step: (0, 0))

    return pl.pallas_call(
        halo_back_kernel,
        grid=(1,),
        out_shape=jax.ShapeDtypeStruct((rows, 3 * width), jnp.bfloat16),
        in_specs=[pl.BlockSpec(memory_space=pltpu.SMEM), whole(own)]
        + [pl.BlockSpec((halo_rows, width), lambda step: (0, 0))]
        + [whole(value) for value in (*pieces, grad_q, part_k, part_v)],
        out_specs=pl.BlockSpec((rows, 3 * width), lambda step: (0, 0)),
        scratch_shapes=[
            pltpu.VMEM((halo_rows, pieces[0].shape[1]), jnp.bfloat16),
            pltpu.VMEM((2 * HEADS, halo_rows), jnp.float32),
        ]
        + [pltpu.VMEM((rows, width), jnp.float32)] * 2,
        compiler_params=pltpu.CompilerParams(vmem_limit_bytes=60 << 20),
        cost_estimate=pl.CostEstimate(
            flops=2 * 4 * 512 * 512 * WIN * HEADS,
            bytes_accessed=20 << 20,
            transcendentals=HEADS * 512 * 512,
        ),
        name="halo_back",
    )(meta, own, halo, *pieces, grad_q, part_k, part_v)


def time_embed(time_index, width):
    half_width = width // 2
    freqs = jnp.exp(-math.log(10000.0) * jnp.arange(half_width, dtype=jnp.float32) / half_width)
    angles = time_index.astype(jnp.float32)[:, None] * freqs[None, :]
    return jnp.concatenate([jnp.cos(angles), jnp.sin(angles)], axis=1)


def layer_norm(value):
    center = value - jnp.mean(value, axis=-1, keepdims=True)
    inverse = lax.rsqrt(jnp.mean(center * center, axis=-1, keepdims=True) + 1e-06)
    return (center * inverse, inverse)


def norm_back(normed, inverse, grad_normed):
    mean_grad = jnp.mean(grad_normed, axis=-1, keepdims=True)
    mean_cross = jnp.mean(grad_normed * normed, axis=-1, keepdims=True)
    return inverse * (grad_normed - mean_grad - normed * mean_cross)


def by_unit(value):
    return value.reshape(-1, UNIT, value.shape[-1])


def per_token(rows):
    units, width = rows.shape
    return jnp.broadcast_to(rows[:, None, :], (units, UNIT, width)).reshape(units * UNIT, width)


def chain(count, step):
    return [(at, at + step) for at in range(count) if 0 <= at + step < count]


def send_halo(own, shards):
    left = lax.ppermute(own, "shard", chain(shards, 1))
    right = lax.ppermute(own, "shard", chain(shards, -1))
    return left, right


def send_far(left, right, shards, step):
    left_far = lax.ppermute(left, "shard", chain(shards, step))
    right_far = lax.ppermute(right, "shard", chain(shards, -step))
    return left_far, right_far


def image_layout(unit_segments, shard):
    units = unit_segments.shape[0]
    first = 2 * shard
    own = lax.dynamic_slice_in_dim(unit_segments, first, 2)
    same = unit_segments[None, :] == own[:, None]
    long = jnp.sum(same, axis=1) > 1
    before = jnp.sum(same[0] & (jnp.arange(units) < first))
    both = long[0] & (own[0] == own[1])
    mode = jnp.where(both, 2, jnp.where(long[0] | long[1], 1, 0))
    which = jnp.where(long[1], 1, 0)
    start = jnp.where(both, 3 - before, jnp.where(long[1], 3, 0))
    slot = start + jnp.arange(3)
    halo_units = jnp.clip(first - 3 + slot + jnp.where(slot >= 3, 2, 0), 0, units - 1)
    meta = jnp.stack([mode, which, start]).astype(jnp.int32)
    return (meta, start, own, unit_segments[halo_units])


def matmul(left, right):
    return jnp.dot(left, right, preferred_element_type=jnp.float32)


def contract_rows(left, right):
    return lax.dot_general(
        left, right, (((0,), (0,)), ((), ())), preferred_element_type=jnp.float32
    )


def contract_cols(left, right):
    return lax.dot_general(
        left, right, (((1,), (1,)), ((), ())), preferred_element_type=jnp.float32
    )


def flipped(mask):
    return [(at, at ^ mask) for at in range(8)]


def swap(value, mask):
    return lax.ppermute(value, "bin", flipped(mask))


def rotate(value, count, step):
    return lax.ppermute(value, "shard", [(at, (at + step) % count) for at in range(count)])


def place_kernel(spots, *refs):
    pieces, out, sems = refs[:-2], refs[-2], refs[-1]
    copies = []
    for at, piece in enumerate(pieces):
        start = pl.multiple_of(spots[at], 16)
        copies.append(
            pltpu.make_async_copy(piece, out.at[pl.ds(start, piece.shape[0])], sems.at[at])
        )
    for copy in copies:
        copy.start()
    for copy in copies:
        copy.wait()


def place_rows(spots, pieces):
    rows = sum(piece.shape[0] for piece in pieces)
    width = pieces[0].shape[1]
    return pl.pallas_call(
        place_kernel,
        out_shape=jax.ShapeDtypeStruct((rows, width), pieces[0].dtype),
        in_specs=[pl.BlockSpec(memory_space=pltpu.SMEM)]
        + [pl.BlockSpec(memory_space=pl.ANY)] * len(pieces),
        out_specs=pl.BlockSpec(memory_space=pl.ANY),
        scratch_shapes=[pltpu.SemaphoreType.DMA((len(pieces),))],
        compiler_params=pltpu.CompilerParams(vmem_limit_bytes=1 << 20),
        cost_estimate=pl.CostEstimate(
            flops=0, bytes_accessed=4 * rows * width, transcendentals=0
        ),
        name="place_rows",
    )(jnp.stack(spots).astype(jnp.int32), *pieces)


def after(value, *others):
    return lax.optimization_barrier((value,) + others)[0]


def together(values, *others):
    return lax.optimization_barrier(tuple(values) + others)[: len(values)]


def rotations(local):
    count = lax.axis_size("shard")
    return [rotate(local, count, step) for step in range(1, count)]


def in_order(local, others):
    count = len(others) + 1
    shard = lax.axis_index("shard")
    ring = jnp.stack(list(others[::-1]) + [local])
    twice = jnp.concatenate([ring, ring])
    return lax.dynamic_slice_in_dim(twice, count - 1 - shard, count)


def columns_of(local, others):
    return in_order(local, others).transpose(1, 0, 2).reshape(local.shape[0], -1)


def row_split(rows):
    return (rows // 2 + 15) // 16 * 16


def place_pieces(pieces, swapped):
    me = lax.axis_index("bin")
    rows = pieces[0].shape[0]
    half = row_split(rows)
    starts = [me, me ^ 2, me ^ 4, me ^ 6, me ^ 6]
    offsets = [0, 0, 0, 0, half]
    spots = [start * rows + offset for start, offset in zip(starts, offsets)]
    spots += [(start ^ 1) * rows + offset for start, offset in zip(starts, offsets)]
    return place_rows(spots, list(pieces) + list(swapped))


def column_parts(short):
    count = lax.axis_size("shard")
    shard = lax.axis_index("shard")
    parts = short.reshape(short.shape[0], count, -1)
    return [
        lax.dynamic_index_in_dim(parts, lax.rem(shard + step, count), 1, keepdims=False)
        for step in range(count)
    ]


def rotate_parts(parts):
    count = len(parts)
    return [rotate(part, count, step) for step, part in enumerate(parts) if step > 0]


def sum_wide(parts):
    return sum(part.astype(jnp.float32) for part in parts)


def scatter_columns(short):
    return lax.psum_scatter(short, "shard", scatter_dimension=1, tiled=True)


def stack_kernel(*refs):
    pieces, out = refs[:-1], refs[-1]
    width = out.shape[1]
    row = 0
    for piece in pieces:
        rows = piece.shape[0]
        for at in range(piece.shape[1] // width):
            out[row : row + rows, :] = piece[:, at * width : (at + 1) * width]
            row += rows


def stack_rows(pieces, width):
    rows = sum(piece.size for piece in pieces) // width
    return pl.pallas_call(
        stack_kernel,
        out_shape=jax.ShapeDtypeStruct((rows, width), pieces[0].dtype),
        in_specs=[pl.BlockSpec(memory_space=pltpu.VMEM)] * len(pieces),
        out_specs=pl.BlockSpec(memory_space=pltpu.VMEM),
        compiler_params=pltpu.CompilerParams(vmem_limit_bytes=8 << 20),
        cost_estimate=pl.CostEstimate(flops=0, bytes_accessed=8 * rows * width, transcendentals=0),
        name="stack_rows",
    )(*pieces)


def add_low(first, second):
    return (first.astype(jnp.float32) + second.astype(jnp.float32)).astype(jnp.bfloat16)


def half_blocks(left):
    me = lax.axis_index("bin")
    turned = lax.optimization_barrier(left.T)
    blocks = turned.reshape(8, turned.shape[0] // 8, -1)
    half = row_split(blocks.shape[1])
    result = []
    for flip in (1, 0):
        own, side, over, cross = [
            lax.dynamic_index_in_dim(blocks, me ^ flip ^ mask, 0, keepdims=False)
            for mask in (0, 2, 4, 6)
        ]
        upper = [part[:half] for part in (own, over, side, cross)]
        lower = [part[half:] for part in (own, side, over, cross)]
        result.append(jnp.concatenate(upper + lower))
    return result


def first_parts(total):
    half = row_split(total.shape[0] // 4)
    rest = total.shape[0] // 4 - half
    return total[2 * half : 4 * half], total[4 * half + 2 * rest :]


def second_parts(total, from_x, from_y):
    half = row_split(total.shape[0] // 4)
    rest = total.shape[0] // 4 - half
    low = 4 * half
    top = total[:half].astype(jnp.float32) + from_x[:half].astype(jnp.float32)
    bottom = total[low : low + rest].astype(jnp.float32) + from_y[:rest].astype(jnp.float32)
    return (
        add_low(total[half : 2 * half], from_x[half:]),
        add_low(total[low + rest : low + 2 * rest], from_y[rest:]),
        top,
        bottom,
    )


def last_rows(top, bottom, upper, lower):
    return jnp.concatenate(
        [top + upper.astype(jnp.float32), bottom + lower.astype(jnp.float32)]
    ).astype(jnp.bfloat16)


def split_low(value):
    high = value.astype(jnp.bfloat16)
    return [high, (value - high.astype(jnp.float32)).astype(jnp.bfloat16)]


def per_device(
    block_input,
    label_embed,
    time_index,
    segment_ids,
    ada_weight,
    ada_bias,
    qkv_weight,
    qv_bias,
    proj_weight,
    proj_bias,
    up_weight,
    up_bias,
    down_weight,
    down_bias,
    bin_weight,
    out_cotangent,
):
    rows, width = block_input.shape
    slots = label_embed.shape[0]
    shards = lax.axis_size("shard")
    bins = lax.axis_size("bin")
    shard = lax.axis_index("shard")
    fast = bins == 8
    unit_segments = segment_ids.reshape(-1, UNIT)[:, 0]
    meta, halo_start, own_segments, halo_segments = image_layout(unit_segments, shard)

    cond = label_embed + time_embed(time_index, width)
    cond_low = jax.nn.silu(cond).astype(jnp.bfloat16)
    modul = matmul(cond_low, ada_weight) + ada_bias
    own_mod = modul[own_segments]
    shift_a, scale_a, gate_a, shift_m, scale_m, gate_m = [
        per_token(part) for part in jnp.split(own_mod, 6, axis=1)
    ]
    halo_mod = modul[halo_segments][:, : 2 * width]
    halo_shift, halo_scale = per_token(halo_mod[:, :width]), per_token(halo_mod[:, width:])

    qkv_parts = rotations(qkv_weight)
    proj_parts = rotations(proj_weight)
    tokens = block_input.astype(jnp.float32)
    normed, inverse = layer_norm(tokens)
    attn_in = (normed * (1.0 + scale_a) + shift_a).astype(jnp.bfloat16)
    qkv_wide = columns_of(qkv_weight, together(qkv_parts, attn_in))
    qkv_full = lax.all_gather(qkv_wide, "bin", axis=0, tiled=True)
    proj_wide = columns_of(proj_weight, together(proj_parts, qkv_wide))
    left, right = send_halo(after(block_input, qkv_wide), shards)
    up_parts = rotations(after(up_weight, qkv_wide))
    if fast:
        proj_x, proj_y = swap(proj_wide, 2), swap(proj_wide, 4)
    else:
        proj_full = lax.all_gather(proj_wide, "bin", axis=0, tiled=True)
    left, right = together((left, right), proj_wide)
    far_left, far_right = together((left[UNIT:], right[:UNIT]))
    up_parts = together(up_parts, far_left, far_right)
    left_far, right_far = send_far(far_left, far_right, shards, 1)
    up_wide = columns_of(up_weight, up_parts)
    up_full = lax.all_gather(up_wide, "bin", axis=0, tiled=True)
    if fast:
        proj_x, proj_y = together((proj_x, proj_y), up_wide)
        half = row_split(proj_wide.shape[0])
        proj_cross = [swap(proj_y[:half], 2), swap(proj_x[half:], 4)]
        proj_core = [swap(piece, 1) for piece in (proj_wide, proj_x, proj_y)]
    qkv_bias = jnp.concatenate([qv_bias[:width], jnp.zeros((width,), jnp.float32), qv_bias[width:]])
    qkv_low = (matmul(after(attn_in, up_wide), qkv_full) + qkv_bias).astype(jnp.bfloat16)
    left_far, right_far = together((left_far, right_far), qkv_low)
    down_parts = rotations(after(down_weight, left_far))
    candidates = jnp.concatenate([left_far, left, right, right_far])
    halo_input = lax.dynamic_slice_in_dim(candidates, halo_start * UNIT, 3 * UNIT)
    halo_normed = layer_norm(halo_input.astype(jnp.float32))[0]
    halo_in = (halo_normed * (1.0 + halo_scale) + halo_shift).astype(jnp.bfloat16)
    halo_low = (matmul(halo_in, qkv_full) + qkv_bias).astype(jnp.bfloat16)
    if fast:
        proj_cross = together(proj_cross, halo_low)
        proj_core += [swap(piece, 1) for piece in proj_cross]
        halo_low = after(halo_low, *proj_cross)
    heads_low, log_total = attend(meta, qkv_low, halo_low)
    down_wide = columns_of(down_weight, together(down_parts, heads_low))
    if fast:
        down_x, down_y = swap(down_wide, 2), swap(down_wide, 4)
        proj_core = together(proj_core, down_wide)
        proj_full = place_pieces([proj_wide, proj_x, proj_y] + list(proj_cross), proj_core)
    else:
        down_full = lax.all_gather(down_wide, "bin", axis=0, tiled=True)
    attn_out = matmul(heads_low, proj_full) + proj_bias
    middle = tokens + gate_a * attn_out
    normed_mlp, inverse_mlp = layer_norm(middle)
    mlp_in = (normed_mlp * (1.0 + scale_m) + shift_m).astype(jnp.bfloat16)
    if fast:
        down_x, down_y = together((down_x, down_y), mlp_in)
        half = row_split(down_wide.shape[0])
        down_cross = together((down_y[:half], down_x[half:]))
        up_full = after(up_full, down_cross[0])
        down_cross = [swap(down_cross[0], 2), swap(down_cross[1], 4)]
        down_core = [swap(piece, 1) for piece in (down_wide, down_x, down_y)]
    pre_act = matmul(mlp_in, up_full) + up_bias
    act_low = lax.optimization_barrier(
        jax.nn.gelu(pre_act, approximate=True).astype(jnp.bfloat16)
    )

    slope = jax.vjp(lambda value: jax.nn.gelu(value, approximate=True), after(pre_act, act_low))[1](
        jnp.ones_like(pre_act)
    )[0]
    slope = lax.optimization_barrier(slope.astype(jnp.bfloat16))

    grad_out = out_cotangent.astype(jnp.float32) * bin_weight[0]
    grad_mlp = (grad_out * gate_m).astype(jnp.bfloat16)
    grad_down = contract_rows(act_low, grad_mlp).astype(jnp.bfloat16)
    if fast:
        down_cross = together(down_cross, grad_down, slope)
        down_core += [swap(piece, 1) for piece in down_cross]
        down_full = place_pieces([down_wide, down_x, down_y] + list(down_cross), down_core)
    grad_mlp = after(grad_mlp, grad_down)
    grad_down = lax.psum_scatter(grad_down, "bin", scatter_dimension=0, tiled=True)
    grad_down_b = jnp.sum(grad_mlp.astype(jnp.float32), axis=0)
    grad_act = contract_cols(grad_mlp, down_full)
    grad_pre = (grad_act * slope.astype(jnp.float32)).astype(jnp.bfloat16)
    grad_up_b = jnp.sum(grad_pre.astype(jnp.float32), axis=0)
    grad_up = contract_rows(mlp_in, grad_pre).astype(jnp.bfloat16)
    grad_in_mlp = contract_cols(after(grad_pre, grad_up), up_full)
    grad_up = lax.psum_scatter(grad_up, "bin", scatter_dimension=0, tiled=True)
    grad_mid = grad_out + norm_back(normed_mlp, inverse_mlp, grad_in_mlp * (1.0 + scale_m))
    grad_attn = (grad_mid * gate_a).astype(jnp.bfloat16)
    grad_proj_b = jnp.sum(grad_attn.astype(jnp.float32), axis=0)
    if fast:
        heads_other, heads_mine = half_blocks(heads_low)
        other_proj = matmul(heads_other, grad_attn).astype(jnp.bfloat16)
        grad_attn = after(grad_attn, other_proj)
        got_proj = swap(other_proj, 1)
    grad_heads = contract_cols(grad_attn, proj_full).astype(jnp.bfloat16)

    lane = jnp.arange(128)[None, :]
    own_head = jnp.arange(width)[:, None] // HEAD_DIM + HEADS == lane % (2 * HEADS)
    own_head &= lane < 4 * HEADS
    delta = jnp.dot(
        grad_heads.astype(jnp.float32) * heads_low.astype(jnp.float32),
        own_head.astype(jnp.float32),
        precision=lax.Precision.HIGHEST,
        preferred_element_type=jnp.float32,
    )
    own_stats = log_total + delta
    high, low = split_low(own_stats)
    payload = jnp.concatenate([grad_heads, jnp.where(lane < 2 * HEADS, high, low)], axis=1)
    left, right = send_halo(payload, shards)
    left_far, right_far = send_far(payload[UNIT:], payload[:UNIT], shards, 2)
    if fast:
        total_proj = matmul(after(heads_mine, payload), grad_attn) + got_proj.astype(jnp.float32)
        total_proj = total_proj.astype(jnp.bfloat16)
        proj_x, proj_y, total_proj = together((*first_parts(total_proj), total_proj))
        grad_heads = after(grad_heads, proj_x, proj_y)
        proj_x, proj_y = swap(proj_x, 2), swap(proj_y, 4)
    else:
        grad_proj = contract_rows(heads_low, grad_attn).astype(jnp.bfloat16)
        grad_proj = lax.psum_scatter(grad_proj, "bin", scatter_dimension=0, tiled=True)
    grad_query, part_keys, part_values = own_back(meta, qkv_low, halo_low, grad_heads, own_stats)
    left, right, left_far, right_far = together((left, right, left_far, right_far), grad_query)
    grad_qkv = halo_back(
        meta,
        qkv_low,
        halo_low,
        (left_far, left, right, right_far),
        grad_query,
        part_keys,
        part_values,
    )
    if fast:
        attn_other, attn_mine = half_blocks(attn_in)
        other_qkv = matmul(attn_other, grad_qkv).astype(jnp.bfloat16)
        got_qkv = swap(other_qkv, 1)
        grad_down_w = scatter_columns(after(grad_down, grad_up, other_qkv))
        grad_up_w = scatter_columns(after(grad_up, other_qkv))
        grad_in_attn = contract_cols(after(grad_qkv, other_qkv), qkv_full)
        total_qkv = matmul(after(attn_mine, grad_in_attn), grad_qkv) + got_qkv.astype(jnp.float32)
        total_qkv = total_qkv.astype(jnp.bfloat16)
        qkv_x, qkv_y, total_qkv = together((*first_parts(total_qkv), total_qkv))
        qkv_x, qkv_y = swap(qkv_x, 2), swap(qkv_y, 4)
        proj_x, proj_y = together((proj_x, proj_y), total_qkv)
        proj_over, proj_side, *proj_kept = second_parts(total_proj, proj_x, proj_y)
        proj_upper, proj_lower = swap(proj_over, 4), swap(proj_side, 2)
        grad_in_attn = after(grad_in_attn, proj_over, proj_side)
    else:
        total_qkv = contract_rows(attn_in, grad_qkv).astype(jnp.bfloat16)
        grad_in_attn = contract_cols(grad_qkv, qkv_full)
    grad_qv_b = jnp.concatenate(
        [
            jnp.sum(grad_qkv[:, :width].astype(jnp.float32), axis=0),
            jnp.sum(grad_qkv[:, 2 * width :].astype(jnp.float32), axis=0),
        ]
    )
    mlp_out = matmul(after(act_low, grad_in_attn), down_full) + down_bias
    result = middle + gate_m * mlp_out
    if fast:
        grad_in_attn = after(grad_in_attn, mlp_out, grad_down_w)
    grad_input = grad_mid + norm_back(normed, inverse, grad_in_attn * (1.0 + scale_a))

    unit_mod = [
        jnp.sum(by_unit(value), axis=1)
        for value in (
            grad_in_attn,
            grad_in_attn * normed,
            grad_mid * attn_out,
            grad_in_mlp,
            grad_in_mlp * normed_mlp,
            grad_out * mlp_out,
        )
    ]
    biases = [part[None, :] for part in (grad_qv_b, grad_proj_b, grad_up_b, grad_down_b)]
    small = stack_rows(unit_mod + biases, width)
    if fast:
        qkv_x, qkv_y = together((qkv_x, qkv_y), small)
        qkv_over, qkv_side, *qkv_kept = second_parts(total_qkv, qkv_x, qkv_y)
        qkv_over, qkv_side = together((qkv_over, qkv_side))
        small = after(small, qkv_over)
        qkv_upper, qkv_lower = swap(qkv_over, 4), swap(qkv_side, 2)
        proj_upper, proj_lower = together((proj_upper, proj_lower), qkv_over)
        grad_proj = last_rows(*proj_kept, proj_upper, proj_lower)
        proj_parts = together(column_parts(grad_proj))
        qkv_upper, qkv_lower = together((qkv_upper, qkv_lower), proj_parts[0])
        grad_qkv_w = last_rows(*qkv_kept, qkv_upper, qkv_lower)
        both_parts = together(
            [
                jnp.concatenate(pair, axis=1)
                for pair in zip(column_parts(grad_qkv_w), proj_parts)
            ]
        )
        both_moved = rotate_parts(both_parts)
        both = sum_wide(list(both_parts[:1]) + both_moved)
        grad_up_w = after(grad_up_w, both)
        grad_qkv_w, grad_proj_w = jnp.split(both, [qkv_weight.shape[1]], axis=1)
    else:
        grad_qkv_w = lax.psum_scatter(total_qkv, "bin", scatter_dimension=0, tiled=True)
        grad_qkv_w, grad_proj_w, grad_up_w, grad_down_w = [
            scatter_columns(part) for part in (grad_qkv_w, grad_proj, grad_up, grad_down)
        ]
    moved = rotations(small)
    small = in_order(small, moved)
    all_units = small[:, :12].reshape(shards, 6, 2, width).transpose(0, 2, 1, 3)
    all_units = all_units.reshape(2 * shards, 6 * width)
    biases = jnp.sum(small[:, 12:], axis=0).reshape(-1)
    picked = unit_segments[None, :] == jnp.arange(slots)[:, None]
    grad_mod = jnp.sum(jnp.where(picked[:, :, None], all_units[None], 0.0), axis=1)
    grad_mod = grad_mod.astype(jnp.bfloat16)
    own_width = grad_mod.shape[1] // (bins * shards)
    mod_view = grad_mod.reshape(slots, bins, shards, own_width)
    mod_columns = lax.dynamic_index_in_dim(mod_view, shard, axis=2, keepdims=False)
    spread = jnp.concatenate(
        [cond_low] + [part.reshape(slots, -1) for part in split_low(biases)], axis=1
    )
    spread = jnp.broadcast_to(spread[:, None, :], (slots, bins, spread.shape[1]))
    traded = lax.all_to_all(
        jnp.concatenate([mod_columns, spread], axis=2),
        "bin",
        split_axis=1,
        concat_axis=0,
        tiled=True,
    )[:, 0]
    grad_cond_act = contract_cols(grad_mod, ada_weight)
    grad_label = jax.vjp(jax.nn.silu, cond)[1](grad_cond_act)[0]
    cond_all = traded[:, own_width : own_width + width]
    grad_ada_w = contract_rows(cond_all, traded[:, :own_width])
    grad_ada_b = jnp.sum(traded[:, :own_width].astype(jnp.float32), axis=0)
    high, lower = jnp.split(traded[:, own_width + width :].astype(jnp.float32), 2, axis=1)
    biases = jnp.sum((high + lower).reshape(bins, -1), axis=0)

    hidden = up_bias.shape[0]
    ends = [2 * width, 3 * width, 3 * width + hidden]
    grad_qv_b, grad_proj_b, grad_up_b, grad_down_b = jnp.split(biases, ends)
    return (
        result,
        grad_input,
        grad_label,
        grad_ada_w,
        grad_ada_b,
        grad_qkv_w.astype(jnp.float32),
        grad_qv_b,
        grad_proj_w.astype(jnp.float32),
        grad_proj_b,
        grad_up_w.astype(jnp.float32),
        grad_up_b,
        grad_down_w.astype(jnp.float32),
        grad_down_b,
    )


def solution(mesh):
    placed = (
        P(("bin", "shard"), None),
        P("bin", None),
        P("bin"),
        P("bin"),
        P(),
        P(),
        P("bin", "shard"),
        P(),
        P("bin", "shard"),
        P(),
        P("bin", "shard"),
        P(),
        P("bin", "shard"),
        P(),
        P("bin"),
        P(("bin", "shard"), None),
    )
    return jax.shard_map(
        per_device,
        mesh=mesh,
        in_specs=placed,
        out_specs=(
            P(("bin", "shard"), None),
            P(("bin", "shard"), None),
            P("bin", None),
            P(None, ("bin", "shard")),
            P(("bin", "shard")),
            P("bin", "shard"),
            P(),
            P("bin", "shard"),
            P(),
            P("bin", "shard"),
            P(),
            P("bin", "shard"),
            P(),
        ),
        check_vma=False,
    )
```
